512 devices in a mesh: tm: 64 (over z_hi, x, y), space: 8 (over z_lo, core).
Axes of the slice: x: 4, y: 8, z: 8 (z_hi: 2, z_lo: 4; z = z_hi * 4 + z_lo), core: 2. Of those that a mesh axis runs over, the one named last changes fastest.
Arguments:
- starts: float32 [64, 16, 96, 128], P('tm', 'space'), may hold values from -1 to 1
Outputs:
- ends: float32 [64, 16, 96, 128], P('tm', 'space')
The draws below stay inside these ranges and needn't reach their ends.
All inputs are finite; a program needn't handle non-finite values.
Results may differ from the reference program's by a relative error of at most 0.00002.
Values sent between devices are 32-bit elements; how exact they have to be, the bound alone decides.
A program may use at most 64 MiB of HBM per device.

```python
import jax
import jax.numpy as jnp
from jax import lax

NY = 96
NX = 128
FSTEPS = 10
CSTEPS = 1
NZ = 16
NT = 64


def block_scale(own_key, extent, shards, least, largest):
    def one(axis_at, blocks):
        draws = jax.random.uniform(jax.random.fold_in(jax.random.fold_in(own_key, 6), axis_at), (blocks,), jnp.float32, least / len(shards), largest / len(shards))
        return jnp.repeat(jnp.exp(draws), extent[axis_at] // blocks).reshape((-1,) + (1,) * (len(extent) - axis_at - 1))

    factor_of = one(*shards[0])
    for cut in shards[1:]:
        factor_of = factor_of * one(*cut)
    return factor_of


def setup_inputs(seed: int = 0) -> dict:
    streams_of = jax.random.split(jax.random.key(seed), 2)
    return {
        "starts": jnp.clip(jax.random.uniform(streams_of[0], (NT, NZ, NY, NX), jnp.float32, -1.0, 1.0) * block_scale(streams_of[0], (NT, NZ, NY, NX), ((0, 64), (1, 8)), -0.4, 0.0), -1.0, 1.0),
    }


def stencil_step(field, rate, react):
    plus_z = jnp.roll(field, -1, 0)
    minus_z = jnp.roll(field, 1, 0)
    plus_y = jnp.roll(field, -1, 1)
    minus_y = jnp.roll(field, 1, 1)
    plus_x = jnp.roll(field, -1, 2)
    minus_x = jnp.roll(field, 1, 2)
    beside = (plus_z + minus_z) + (plus_y + minus_y) + (plus_x + minus_x)
    return field + rate * (beside - 6.0 * field) + react * (field - field * field * field)


def fine_map(field):
    for count in range(FSTEPS):
        field = stencil_step(field, 0.03, 0.02)
    return field


def coarse_map(field):
    for count in range(CSTEPS):
        field = stencil_step(field, 0.15, 0.1)
    return field


def reference(starts):
    fine = jax.vmap(fine_map)(starts)
    delta = fine - jax.vmap(coarse_map)(starts)

    def advance(carried, piece):
        result = coarse_map(carried) + piece
        return result, result

    final, ends = lax.scan(advance, starts[0], delta)
    return ends
```

```python
import jax
import jax.numpy as jnp
from jax import lax
from jax.experimental import pallas as pl
from jax.experimental.pallas import tpu as pltpu
from jax.sharding import PartitionSpec as P

MESH = pl.DeviceIdType.MESH
FSTEPS = 10
GROUP = 16
TILE = 12
WIDE = TILE + 2 * FSTEPS
SPAN = TILE + 2 * GROUP
REACH = (12, 12, 8, 4)


def step(src, dst, first, last, rate, react, more=None, keep=None):
    stay = 1.0 - 6.0 * rate + react
    halves = (slice(0, 8), slice(8, 16))
    below = [src[first - 1, h] for h in halves]
    here = [src[first, h] for h in halves]
    for y in range(first, last):
        above = [src[y + 1, h] for h in halves]
        for h, turn in ((0, 1), (1, 7)):
            v, other = here[h], here[1 - h]
            beside = (
                (other + pltpu.roll(other, turn, 0))
                + (below[h] + above[h])
                + (pltpu.roll(v, 1, 1) + pltpu.roll(v, 127, 1))
            )
            out = v * (stay - react * (v * v)) + rate * beside
            if more is not None:
                out = out + more(y, halves[h])
            dst[y, halves[h]] = out
            if keep is not None:
                keep(y, h, out)
        below, here = here, above


def kernel(
    x_ref, o_ref, wrapped, gathered, u, v, base, deltas_own, deltas, s, c, out_rows,
    slab_send, slab_recv, spread_send, delta_recv, state_recv, ends_send, ends_recv,
):
    n, sp = lax.axis_index("tm"), lax.axis_index("space")
    group, k_own = n // GROUP, n % GROUP
    quarter = k_own // 4

    def chain_tm(g, tile):
        return g * GROUP + (1 - g % 2) * 8 + tile

    is_chain = n == chain_tm(group, sp)

    wrapped[:, FSTEPS : FSTEPS + 96] = x_ref[0]
    wrapped[:, 0:FSTEPS] = x_ref[0, :, 96 - FSTEPS : 96]
    wrapped[:, FSTEPS + 96 : 2 * FSTEPS + 96] = x_ref[0, :, 0:FSTEPS]
    copies = []
    for j in range(1, 8):
        to = (sp + j) % 8
        cp = pltpu.make_async_remote_copy(
            src_ref=wrapped.at[:, pl.ds(TILE * to, WIDE)],
            dst_ref=gathered.at[pl.ds(2 * sp, 2)],
            send_sem=slab_send.at[j],
            recv_sem=slab_recv.at[j],
            device_id=(n, to),
            device_id_type=MESH,
        )
        cp.start()
        copies.append(cp)
    own = pltpu.make_async_copy(
        wrapped.at[:, pl.ds(TILE * sp, WIDE)], gathered.at[pl.ds(2 * sp, 2)], slab_recv.at[0]
    )
    own.start()
    own.wait()
    for cp in copies:
        cp.wait_recv()

    flat = gathered.reshape(16 * WIDE, 128)
    for y in range(WIDE):
        u[y, 0:8] = flat[pl.ds(y, 8, stride=2 * WIDE), :]
        u[y, 8:16] = flat[pl.ds(WIDE + y, 8, stride=2 * WIDE), :]
    first, last = FSTEPS, FSTEPS + TILE
    base[...] = u[first:last]
    step(u, v, first, last, 0.15, 0.1)
    deltas_own[...] = v[first:last]
    a, b = u, v
    for i in range(FSTEPS):
        step(a, b, i + 1, WIDE - 1 - i, 0.03, 0.02)
        a, b = b, a
    deltas_own[...] = a[first:last] - deltas_own[...]

    def spread(src, dst_of, recv, g, reach, far, sends, act):
        parts = [(0, 0, TILE, GROUP)]
        parts += [(1, TILE - reach, reach, GROUP - reach), (7, 0, reach, GROUP + TILE)]
        if far:
            parts += [(2, TILE - far, far, 0), (6, 0, far, GROUP + 2 * TILE)]
        for j, (off, at, rows, to) in enumerate(parts):
            tile = (sp + off) % 8
            tm = chain_tm(g, tile)
            src_part, dst_part = src.at[pl.ds(at, rows)], dst_of.at[pl.ds(to, rows)]
            far_copy = pltpu.make_async_remote_copy(
                src_ref=src_part,
                dst_ref=dst_part,
                send_sem=spread_send.at[sends, j],
                recv_sem=recv,
                device_id=(tm, tile),
                device_id_type=MESH,
            )
            if off:
                act(far_copy)
            else:
                mine = tm == n

                @pl.when(jnp.logical_not(mine))
                def _():
                    act(far_copy)

                if act is start:

                    @pl.when(mine)
                    def _():
                        pltpu.make_async_copy(src_part, dst_part, recv).start()

    def start(cp):
        cp.start()

    def finish(cp):
        cp.wait_send()

    def spread_deltas(act):
        for q in range(4):

            @pl.when(quarter == q)
            def _():
                spread(
                    deltas_own, deltas.at[k_own], delta_recv.at[k_own],
                    group, REACH[q], 4 if q == 0 else 0, 0, act,
                )

    def spread_first(act):
        @pl.when(n == 0)
        def _():
            spread(base, s, state_recv, 0, 12, 4, 1, act)

    spread_first(start)
    spread_deltas(start)
    spread_first(finish)
    spread_deltas(finish)

    flat_out = out_rows.reshape(GROUP * 16 * 16, 128)

    @pl.when(is_chain)
    def _():
        pltpu.make_async_copy(s, s, state_recv).wait()
        for q in range(4):
            rows = TILE + 2 * REACH[q] + (8 if q == 0 else 0)

            def pair(i, _, q=q, rows=rows):
                for half, (src, dst) in enumerate(((s, c), (c, s))):
                    k = 4 * q + 2 * i + half
                    whole = deltas.at[k, pl.ds(0, rows)]
                    pltpu.make_async_copy(whole, whole, delta_recv.at[k]).wait()

                    def keep(y, h, out):
                        if GROUP <= y < GROUP + TILE:
                            flat_out[pl.ds(k * 256 + 16 * h + y - GROUP, 8, stride=32), :] = out

                    step(
                        src, dst, 4 * q + 1, SPAN - 1 - 4 * q, 0.15, 0.1,
                        lambda y, h: deltas[k, y, h], keep,
                    )
                return 0

            lax.fori_loop(0, 2, pair, 0)

        mid = s.at[pl.ds(GROUP, TILE)]

        def pass_on(act):
            @pl.when(group < 3)
            def _():
                spread(mid, s, state_recv, group + 1, 12, 4, 1, act)

        pass_on(start)

        def send(i, _):
            k, to = i // 8, i % 8
            tm = group * GROUP + k
            src = out_rows.at[pl.ds(16 * k + 2 * to, 2), pl.ds(0, TILE)]
            dst = o_ref.at[0, :, pl.ds(TILE * sp, TILE)]
            mine = jnp.logical_and(tm == n, to == sp)

            @pl.when(mine)
            def _():
                pltpu.make_async_copy(src, dst, ends_recv).start()

            @pl.when(jnp.logical_not(mine))
            def _():
                pltpu.make_async_remote_copy(
                    src_ref=src,
                    dst_ref=dst,
                    send_sem=ends_send,
                    recv_sem=ends_recv,
                    device_id=(tm, to),
                    device_id_type=MESH,
                ).start()

            return 0

        lax.fori_loop(0, 8 * GROUP, send, 0)
        pass_on(finish)
        sent = out_rows.at[pl.ds(0, 2 * (8 * GROUP - 1)), pl.ds(0, TILE)]
        pltpu.make_async_copy(sent, sent, ends_send).wait()

    for cp in copies:
        cp.wait_send()
    pltpu.make_async_copy(o_ref, o_ref, ends_recv).wait()


def per_device(starts):
    field = jnp.float32
    dma = pltpu.SemaphoreType.DMA
    return pl.pallas_call(
        kernel,
        out_shape=jax.ShapeDtypeStruct(starts.shape, starts.dtype),
        in_specs=[pl.BlockSpec(memory_space=pltpu.VMEM)],
        out_specs=pl.BlockSpec(memory_space=pl.ANY),
        scratch_shapes=[
            pltpu.VMEM((2, 96 + 2 * FSTEPS, 128), field),
            pltpu.VMEM((16, WIDE, 128), field),
            pltpu.VMEM((WIDE, 16, 128), field),
            pltpu.VMEM((WIDE, 16, 128), field),
            pltpu.VMEM((TILE, 16, 128), field),
            pltpu.VMEM((TILE, 16, 128), field),
            pltpu.VMEM((GROUP, SPAN, 16, 128), field),
            pltpu.VMEM((SPAN, 16, 128), field),
            pltpu.VMEM((SPAN, 16, 128), field),
            pltpu.VMEM((GROUP * 16, 16, 128), field),
            dma((8,)),
            dma((8,)),
            dma((2, 5)),
            dma((GROUP,)),
            dma,
            dma,
            dma,
        ],
        compiler_params=pltpu.CompilerParams(has_side_effects=True, vmem_limit_bytes=40 << 20),
    )(starts)


def solution(mesh):
    placed = P("tm", "space", None, None)
    return jax.shard_map(
        per_device, mesh=mesh, in_specs=(placed,), out_specs=placed, check_vma=False
    )
```

```python
import jax
import jax.numpy as jnp
from jax import lax
from jax.experimental import pallas as pl
from jax.experimental.pallas import tpu as pltpu
from jax.sharding import PartitionSpec as P

MESH = pl.DeviceIdType.MESH
FSTEPS = 10
STARTS = (0, 8, 20, 40, 64)
BLOCKS = len(STARTS) - 1
SIZES = tuple(STARTS[b + 1] - STARTS[b] for b in range(BLOCKS))
GHOST = max(SIZES)
TILE = 12
WIDE = TILE + 2 * FSTEPS
SPAN = TILE + 2 * GHOST


def step(src, dst, first, last, rate, react, more=None, keep=None):
    stay = 1.0 - 6.0 * rate + react
    halves = (slice(0, 8), slice(8, 16))
    below = [src[first - 1, h] for h in halves]
    here = [src[first, h] for h in halves]
    for y in range(first, last):
        above = [src[y + 1, h] for h in halves]
        for h, turn in ((0, 1), (1, 7)):
            v, other = here[h], here[1 - h]
            beside = (
                (other + pltpu.roll(other, turn, 0))
                + (below[h] + above[h])
                + (pltpu.roll(v, 1, 1) + pltpu.roll(v, 127, 1))
            )
            out = v * (stay - react * (v * v)) + rate * beside
            if more is not None:
                out = out + more(y, halves[h])
            dst[y, halves[h]] = out
            if keep is not None:
                keep(y, h, out)
        below, here = here, above


def tile_of(sp):
    z = sp // 2
    return jnp.where(sp % 2 == 0, z, 7 - z)


def space_of(tile):
    return jnp.where(tile < 4, 2 * tile, 2 * (7 - tile) + 1)


def chain_tm(block, tile):
    return block * 16 + (tile % 2) * 8


def table(values, at):
    out = values[0]
    for i in range(1, len(values)):
        out = jnp.where(at >= i, values[i], out)
    return out


def kernel(
    x_ref, o_ref, wrapped, gathered, u, v, base, deltas_own, deltas, s, c, out_rows,
    slab_send, slab_recv, spread_send, delta_recv, state_recv, ends_send, ends_recv,
):
    n, sp = lax.axis_index("tm"), lax.axis_index("space")
    tile = tile_of(sp)
    block = sum((n >= start).astype(jnp.int32) for start in STARTS[1:BLOCKS])
    left = table(STARTS[1:], block) - 1 - n
    hub = chain_tm(block, tile)
    chain_block = n // 16
    is_chain = n == chain_tm(chain_block, tile)
    chain_start = table(STARTS, chain_block)
    chain_size = table(SIZES, chain_block)
    chain_in_own = jnp.logical_and(n >= chain_start, n < chain_start + chain_size)

    barrier = pltpu.get_barrier_semaphore()

    def greet(tm, space):
        pl.semaphore_signal(barrier, inc=1, device_id=(tm, space), device_id_type=MESH)

    for j in range(1, 8):
        greet(n, (sp + j) % 8)
    is_hub = hub == n

    @pl.when(jnp.logical_not(is_hub))
    def _():
        greet(hub, sp)

    @pl.when(is_chain)
    def _():
        def spoke(i, _):
            @pl.when(chain_start + i != n)
            def _():
                greet(chain_start + i, sp)

            return 0

        lax.fori_loop(0, chain_size, spoke, 0)

        @pl.when(chain_block > 0)
        def _():
            for off in (-2, -1, 0, 1, 2):
                other = (tile + off) % 8
                greet(chain_tm(chain_block - 1, other), space_of(other))

    expected = 7 + jnp.where(is_hub, 0, 1)
    spokes = chain_size - jnp.where(chain_in_own, 1, 0) + jnp.where(chain_block < BLOCKS - 1, 5, 0)
    pl.semaphore_wait(barrier, expected + jnp.where(is_chain, spokes, 0))

    wrapped[:, FSTEPS : FSTEPS + 96] = x_ref[0]
    wrapped[:, 0:FSTEPS] = x_ref[0, :, 96 - FSTEPS : 96]
    wrapped[:, FSTEPS + 96 : 2 * FSTEPS + 96] = x_ref[0, :, 0:FSTEPS]
    copies = []
    for j in range(1, 8):
        to = (sp + j) % 8
        cp = pltpu.make_async_remote_copy(
            src_ref=wrapped.at[:, pl.ds(TILE * tile_of(to), WIDE)],
            dst_ref=gathered.at[pl.ds(2 * sp, 2)],
            send_sem=slab_send.at[j],
            recv_sem=slab_recv.at[j],
            device_id=(n, to),
            device_id_type=MESH,
        )
        cp.start()
        copies.append(cp)
    own = pltpu.make_async_copy(
        wrapped.at[:, pl.ds(TILE * tile, WIDE)], gathered.at[pl.ds(2 * sp, 2)], slab_recv.at[0]
    )
    own.start()
    own.wait()
    for cp in copies:
        cp.wait_recv()

    flat = gathered.reshape(16 * WIDE, 128)
    for y in range(WIDE):
        u[y, 0:8] = flat[pl.ds(y, 8, stride=2 * WIDE), :]
        u[y, 8:16] = flat[pl.ds(WIDE + y, 8, stride=2 * WIDE), :]
    first, last = FSTEPS, FSTEPS + TILE
    base[...] = u[first:last]
    step(u, v, first, last, 0.15, 0.1)
    deltas_own[...] = v[first:last]
    a, b = u, v
    for i in range(FSTEPS):
        step(a, b, i + 1, WIDE - 1 - i, 0.03, 0.02)
        a, b = b, a
    deltas_own[...] = a[first:last] - deltas_own[...]

    def spread(src, dst_of, recv, to_block, ghost, sends, act):
        near, far = min(ghost, TILE), max(ghost - TILE, 0)
        parts = [(1, TILE - near, near, GHOST - near), (7, 0, near, GHOST + TILE), (0, 0, TILE, GHOST)]
        if far:
            parts = [(2, TILE - far, far, GHOST - TILE - far), (6, 0, far, GHOST + 2 * TILE)] + parts
        for off, at, rows, to in parts:
            dest = (tile + off) % 8
            tm, space = chain_tm(to_block, dest), space_of(dest)
            src_part, dst_part = src.at[pl.ds(at, rows)], dst_of.at[pl.ds(to, rows)]
            far_copy = pltpu.make_async_remote_copy(
                src_ref=src_part,
                dst_ref=dst_part,
                send_sem=spread_send.at[sends, off],
                recv_sem=recv,
                device_id=(tm, space),
                device_id_type=MESH,
            )
            if off:
                act(far_copy)
            else:
                mine = tm == n

                @pl.when(jnp.logical_not(mine))
                def _():
                    act(far_copy)

                if act is start:

                    @pl.when(mine)
                    def _():
                        pltpu.make_async_copy(src_part, dst_part, recv).start()

    def start(cp):
        cp.start()

    def finish(cp):
        cp.wait_send()

    def spread_deltas(act):
        for q in range(GHOST // 4):

            @pl.when(left // 4 == q)
            def _():
                spread(
                    deltas_own, deltas.at[left], delta_recv.at[left], block, 4 * q + 4, 0, act
                )

    def spread_first(act):
        @pl.when(n == 0)
        def _():
            spread(base, s, state_recv, 0, SIZES[0], 1, act)

    spread_first(start)
    spread_deltas(start)
    spread_first(finish)
    spread_deltas(finish)

    flat_out = out_rows.reshape(GHOST * 16 * 16, 128)

    @pl.when(is_chain)
    def _():
        for b in range(BLOCKS):

            @pl.when(chain_block == b)
            def _():
                whole = s.at[pl.ds(0, TILE + 2 * SIZES[b])]
                pltpu.make_async_copy(whole, whole, state_recv).wait()

        for q in reversed(range(GHOST // 4)):
            ghost = 4 * q + 4

            def pair(i, _, ghost=ghost):
                for half, (src, dst) in enumerate(((s, c), (c, s))):
                    rem = ghost - 1 - 2 * i - half
                    whole = deltas.at[rem, pl.ds(0, TILE + 2 * ghost)]
                    pltpu.make_async_copy(whole, whole, delta_recv.at[rem]).wait()

                    def keep(y, h, out):
                        if GHOST <= y < GHOST + TILE:
                            flat_out[pl.ds(rem * 256 + 16 * h + y - GHOST, 8, stride=32), :] = out

                    step(
                        src, dst, GHOST + 1 - ghost, GHOST + TILE + ghost - 1, 0.15, 0.1,
                        lambda y, h: deltas[rem, y, h], keep,
                    )
                return 0

            lax.fori_loop(0, jnp.where(chain_size >= ghost, 2, 0), pair, 0)

        mid = s.at[pl.ds(GHOST, TILE)]

        def pass_on(act):
            for b in range(BLOCKS - 1):

                @pl.when(chain_block == b)
                def _():
                    spread(mid, s, state_recv, b + 1, SIZES[b + 1], 1, act)

        pass_on(start)

        def send(i, _):
            rem, to = chain_size - 1 - i // 8, i % 8
            tm = chain_start + i // 8
            src = out_rows.at[pl.ds(16 * rem + 2 * to, 2), pl.ds(0, TILE)]
            dst = o_ref.at[0, :, pl.ds(TILE * tile, TILE)]
            mine = jnp.logical_and(tm == n, to == sp)

            @pl.when(mine)
            def _():
                pltpu.make_async_copy(src, dst, ends_recv).start()

            @pl.when(jnp.logical_not(mine))
            def _():
                pltpu.make_async_remote_copy(
                    src_ref=src,
                    dst_ref=dst,
                    send_sem=ends_send,
                    recv_sem=ends_recv,
                    device_id=(tm, to),
                    device_id_type=MESH,
                ).start()

            return 0

        lax.fori_loop(0, 8 * chain_size, send, 0)
        pass_on(finish)
        for b in range(BLOCKS):
            for own in (False, True):

                @pl.when(jnp.logical_and(chain_block == b, chain_in_own == own))
                def _():
                    sent = out_rows.at[pl.ds(0, 2 * (8 * SIZES[b] - own)), pl.ds(0, TILE)]
                    pltpu.make_async_copy(sent, sent, ends_send).wait()

    for cp in copies:
        cp.wait_send()
    pltpu.make_async_copy(o_ref, o_ref, ends_recv).wait()


def per_device(starts):
    field = jnp.float32
    dma = pltpu.SemaphoreType.DMA
    return pl.pallas_call(
        kernel,
        out_shape=jax.ShapeDtypeStruct(starts.shape, starts.dtype),
        in_specs=[pl.BlockSpec(memory_space=pltpu.VMEM)],
        out_specs=pl.BlockSpec(memory_space=pl.ANY),
        scratch_shapes=[
            pltpu.VMEM((2, 96 + 2 * FSTEPS, 128), field),
            pltpu.VMEM((16, WIDE, 128), field),
            pltpu.VMEM((WIDE, 16, 128), field),
            pltpu.VMEM((WIDE, 16, 128), field),
            pltpu.VMEM((TILE, 16, 128), field),
            pltpu.VMEM((TILE, 16, 128), field),
            pltpu.VMEM((GHOST, SPAN, 16, 128), field),
            pltpu.VMEM((SPAN, 16, 128), field),
            pltpu.VMEM((SPAN, 16, 128), field),
            pltpu.VMEM((GHOST * 16, 16, 128), field),
            dma((8,)),
            dma((8,)),
            dma((2, 8)),
            dma((GHOST,)),
            dma,
            dma,
            dma,
        ],
        compiler_params=pltpu.CompilerParams(
            collective_id=0, has_side_effects=True, vmem_limit_bytes=40 << 20
        ),
    )(starts)


def solution(mesh):
    placed = P("tm", "space", None, None)
    return jax.shard_map(
        per_device, mesh=mesh, in_specs=(placed,), out_specs=placed, check_vma=False
    )
```

```python
import jax
import jax.numpy as jnp
from jax import lax
from jax.experimental import pallas as pl
from jax.experimental.pallas import tpu as pltpu
from jax.sharding import PartitionSpec as P

MESH = pl.DeviceIdType.MESH
FSTEPS = 10
STARTS = (0, 8, 20, 32, 48, 64)
BLOCKS = len(STARTS) - 1
SIZES = tuple(STARTS[b + 1] - STARTS[b] for b in range(BLOCKS))
GHOST = max(SIZES)
BASES = (0, 8, 24, 32, 56)
TILE = 12
WIDE = TILE + 2 * FSTEPS
SPAN = TILE + 2 * GHOST


def step(src, dst, first, last, rate, react, more=None, keep=None):
    stay = 1.0 - 6.0 * rate + react
    halves = (slice(0, 8), slice(8, 16))
    below = [src[first - 1, h] for h in halves]
    here = [src[first, h] for h in halves]
    for y in range(first, last):
        above = [src[y + 1, h] for h in halves]
        for h, turn in ((0, 1), (1, 7)):
            v, other = here[h], here[1 - h]
            beside = (
                (other + pltpu.roll(other, turn, 0))
                + (below[h] + above[h])
                + (pltpu.roll(v, 1, 1) + pltpu.roll(v, 127, 1))
            )
            out = v * (stay - react * (v * v)) + rate * beside
            if more is not None:
                out = out + more(y, halves[h])
            dst[y, halves[h]] = out
            if keep is not None:
                keep(y, h, out)
        below, here = here, above


def tile_of(sp, tm):
    z = jnp.where(tm < 32, sp // 2, 3 - sp // 2)
    return jnp.where(sp % 2 == 0, z, 7 - z)


def space_of(tile, tm):
    z = jnp.where(tile < 4, tile, 7 - tile)
    return 2 * jnp.where(tm < 32, z, 3 - z) + jnp.where(tile < 4, 0, 1)


def table(values, at):
    out = values[0]
    for i in range(1, len(values)):
        out = jnp.where(at >= i, values[i], out)
    return out


def kernel(
    x_ref, o_ref, wrapped, gathered, u, v, base, deltas_own, deltas, s, c, out_rows,
    slab_send, slab_recv, spread_send, delta_recv, state_recv, ends_send, ends_recv,
):
    n, sp = lax.axis_index("tm"), lax.axis_index("space")
    tile = tile_of(sp, n)
    block = sum((n >= start).astype(jnp.int32) for start in STARTS[1:BLOCKS])
    left = table(STARTS[1:], block) - 1 - n
    hub = table(BASES, block) + tile
    is_chain = hub == n
    size = table(SIZES, block)
    first_slice = table(STARTS, block)

    barrier = pltpu.get_barrier_semaphore()

    def greet(tm, space):
        pl.semaphore_signal(barrier, inc=1, device_id=(tm, space), device_id_type=MESH)

    for j in range(1, 8):
        greet(n, (sp + j) % 8)

    @pl.when(jnp.logical_not(is_chain))
    def _():
        greet(hub, sp)

    @pl.when(is_chain)
    def _():
        def spoke(i, _):
            @pl.when(first_slice + i != n)
            def _():
                greet(first_slice + i, sp)

            return 0

        lax.fori_loop(0, size, spoke, 0)

        @pl.when(block > 0)
        def _():
            before = table(BASES, block - 1)
            for off in (-2, -1, 0, 1, 2):
                other = (tile + off) % 8
                greet(before + other, space_of(other, before))

    spokes = size - 1 + jnp.where(block < BLOCKS - 1, 5, 0)
    pl.semaphore_wait(barrier, 7 + jnp.where(is_chain, spokes, 1))

    wrapped[:, FSTEPS : FSTEPS + 96] = x_ref[0]
    wrapped[:, 0:FSTEPS] = x_ref[0, :, 96 - FSTEPS : 96]
    wrapped[:, FSTEPS + 96 : 2 * FSTEPS + 96] = x_ref[0, :, 0:FSTEPS]
    copies = []
    for j in range(1, 8):
        to = (sp + j) % 8
        cp = pltpu.make_async_remote_copy(
            src_ref=wrapped.at[:, pl.ds(TILE * tile_of(to, n), WIDE)],
            dst_ref=gathered.at[pl.ds(2 * sp, 2)],
            send_sem=slab_send.at[j],
            recv_sem=slab_recv.at[j],
            device_id=(n, to),
            device_id_type=MESH,
        )
        cp.start()
        copies.append(cp)
    own = pltpu.make_async_copy(
        wrapped.at[:, pl.ds(TILE * tile, WIDE)], gathered.at[pl.ds(2 * sp, 2)], slab_recv.at[0]
    )
    own.start()
    own.wait()
    for cp in copies:
        cp.wait_recv()

    flat = gathered.reshape(16 * WIDE, 128)
    for y in range(WIDE):
        u[y, 0:8] = flat[pl.ds(y, 8, stride=2 * WIDE), :]
        u[y, 8:16] = flat[pl.ds(WIDE + y, 8, stride=2 * WIDE), :]
    first, last = FSTEPS, FSTEPS + TILE
    base[...] = u[first:last]
    step(u, v, first, last, 0.15, 0.1)
    deltas_own[...] = v[first:last]
    a, b = u, v
    for i in range(FSTEPS):
        step(a, b, i + 1, WIDE - 1 - i, 0.03, 0.02)
        a, b = b, a
    deltas_own[...] = a[first:last] - deltas_own[...]

    def spread(src, dst_of, recv, base_tm, ghost, sends, act):
        near, far = min(ghost, TILE), max(ghost - TILE, 0)
        parts = [(1, TILE - near, near, GHOST - near), (7, 0, near, GHOST + TILE), (0, 0, TILE, GHOST)]
        if far:
            parts = [(2, TILE - far, far, GHOST - TILE - far), (6, 0, far, GHOST + 2 * TILE)] + parts
        for off, at, rows, to in parts:
            dest = (tile + off) % 8
            tm, space = base_tm + dest, space_of(dest, base_tm)
            src_part, dst_part = src.at[pl.ds(at, rows)], dst_of.at[pl.ds(to, rows)]
            far_copy = pltpu.make_async_remote_copy(
                src_ref=src_part,
                dst_ref=dst_part,
                send_sem=spread_send.at[sends, off],
                recv_sem=recv,
                device_id=(tm, space),
                device_id_type=MESH,
            )
            if off:
                act(far_copy)
            else:
                mine = tm == n

                @pl.when(jnp.logical_not(mine))
                def _():
                    act(far_copy)

                if act is start:

                    @pl.when(mine)
                    def _():
                        pltpu.make_async_copy(src_part, dst_part, recv).start()

    def start(cp):
        cp.start()

    def finish(cp):
        cp.wait_send()

    def spread_deltas(act):
        for q in range(GHOST // 4):

            @pl.when(left // 4 == q)
            def _():
                spread(
                    deltas_own, deltas.at[left], delta_recv.at[left],
                    table(BASES, block), 4 * q + 4, 0, act,
                )

    def spread_first(act):
        @pl.when(n == 0)
        def _():
            spread(base, s, state_recv, BASES[0], SIZES[0], 1, act)

    spread_first(start)
    spread_deltas(start)
    spread_first(finish)
    spread_deltas(finish)

    flat_out = out_rows.reshape(GHOST * 16 * 16, 128)

    @pl.when(is_chain)
    def _():
        for b in range(BLOCKS):

            @pl.when(block == b)
            def _():
                whole = s.at[pl.ds(0, TILE + 2 * SIZES[b])]
                pltpu.make_async_copy(whole, whole, state_recv).wait()

        for q in reversed(range(GHOST // 4)):
            ghost = 4 * q + 4

            def pair(i, _, ghost=ghost):
                for half, (src, dst) in enumerate(((s, c), (c, s))):
                    rem = ghost - 1 - 2 * i - half
                    whole = deltas.at[rem, pl.ds(0, TILE + 2 * ghost)]
                    pltpu.make_async_copy(whole, whole, delta_recv.at[rem]).wait()

                    def keep(y, h, out):
                        if GHOST <= y < GHOST + TILE:
                            flat_out[pl.ds(rem * 256 + 16 * h + y - GHOST, 8, stride=32), :] = out

                    step(
                        src, dst, GHOST + 1 - ghost, GHOST + TILE + ghost - 1, 0.15, 0.1,
                        lambda y, h: deltas[rem, y, h], keep,
                    )
                return 0

            lax.fori_loop(0, jnp.where(size >= ghost, 2, 0), pair, 0)

        mid = s.at[pl.ds(GHOST, TILE)]

        def pass_on(act):
            for b in range(BLOCKS - 1):

                @pl.when(block == b)
                def _():
                    spread(mid, s, state_recv, BASES[b + 1], SIZES[b + 1], 1, act)

        pass_on(start)

        def send(i, _):
            rem, to = size - 1 - i // 8, i % 8
            tm = first_slice + i // 8
            src = out_rows.at[pl.ds(16 * rem + 2 * to, 2), pl.ds(0, TILE)]
            dst = o_ref.at[0, :, pl.ds(TILE * tile, TILE)]
            mine = jnp.logical_and(tm == n, to == sp)

            @pl.when(mine)
            def _():
                pltpu.make_async_copy(src, dst, ends_recv).start()

            @pl.when(jnp.logical_not(mine))
            def _():
                pltpu.make_async_remote_copy(
                    src_ref=src,
                    dst_ref=dst,
                    send_sem=ends_send,
                    recv_sem=ends_recv,
                    device_id=(tm, to),
                    device_id_type=MESH,
                ).start()

            return 0

        lax.fori_loop(0, 8 * size, send, 0)
        pass_on(finish)
        for b in range(BLOCKS):

            @pl.when(block == b)
            def _():
                sent = out_rows.at[pl.ds(0, 2 * (8 * SIZES[b] - 1)), pl.ds(0, TILE)]
                pltpu.make_async_copy(sent, sent, ends_send).wait()

    for cp in copies:
        cp.wait_send()
    pltpu.make_async_copy(o_ref, o_ref, ends_recv).wait()


def per_device(starts):
    field = jnp.float32
    dma = pltpu.SemaphoreType.DMA
    return pl.pallas_call(
        kernel,
        out_shape=jax.ShapeDtypeStruct(starts.shape, starts.dtype),
        in_specs=[pl.BlockSpec(memory_space=pltpu.VMEM)],
        out_specs=pl.BlockSpec(memory_space=pl.ANY),
        scratch_shapes=[
            pltpu.VMEM((2, 96 + 2 * FSTEPS, 128), field),
            pltpu.VMEM((16, WIDE, 128), field),
            pltpu.VMEM((WIDE, 16, 128), field),
            pltpu.VMEM((WIDE, 16, 128), field),
            pltpu.VMEM((TILE, 16, 128), field),
            pltpu.VMEM((TILE, 16, 128), field),
            pltpu.VMEM((GHOST, SPAN, 16, 128), field),
            pltpu.VMEM((SPAN, 16, 128), field),
            pltpu.VMEM((SPAN, 16, 128), field),
            pltpu.VMEM((GHOST * 16, 16, 128), field),
            dma((8,)),
            dma((8,)),
            dma((2, 8)),
            dma((GHOST,)),
            dma,
            dma,
            dma,
        ],
        compiler_params=pltpu.CompilerParams(
            collective_id=0, has_side_effects=True, vmem_limit_bytes=40 << 20
        ),
    )(starts)


def solution(mesh):
    placed = P("tm", "space", None, None)
    return jax.shard_map(
        per_device, mesh=mesh, in_specs=(placed,), out_specs=placed, check_vma=False
    )
```

```python
import functools

import jax
import jax.numpy as jnp
from jax import lax
from jax.experimental import pallas as pl
from jax.experimental.pallas import tpu as pltpu
from jax.sharding import PartitionSpec as P

MESH = pl.DeviceIdType.MESH
FSTEPS = 10
STARTS = (0, 8, 20, 32, 48, 64)
BLOCKS = len(STARTS) - 1
SIZES = tuple(STARTS[b + 1] - STARTS[b] for b in range(BLOCKS))
GHOST = max(SIZES)
PLACES = ((0, 0), (8, 8), (24, 24), (32, 40), (56, 48))
TILE = 12
WIDE = TILE + 2 * FSTEPS
SPAN = TILE + 2 * GHOST


def step(src, dst, first, last, rate, react, more=None, keep=None):
    stay = 1.0 - 6.0 * rate + react
    halves = (slice(0, 8), slice(8, 16))
    below = [src[first - 1, h] for h in halves]
    here = [src[first, h] for h in halves]
    for y in range(first, last):
        above = [src[y + 1, h] for h in halves]
        for h, turn in ((0, 1), (1, 7)):
            v, other = here[h], here[1 - h]
            beside = (
                (other + pltpu.roll(other, turn, 0))
                + (below[h] + above[h])
                + (pltpu.roll(v, 1, 1) + pltpu.roll(v, 127, 1))
            )
            out = v * (stay - react * (v * v)) + rate * beside
            if more is not None:
                out = out + more(y, halves[h])
            dst[y, halves[h]] = out
            if keep is not None:
                keep(y, h, out)
        below, here = here, above


def tile_of(sp, tm):
    z = jnp.where(tm < 32, sp // 2, 3 - sp // 2)
    return jnp.where(sp % 2 == 0, z, 7 - z)


def space_of(tile, tm):
    z = jnp.where(tile < 4, tile, 7 - tile)
    return 2 * jnp.where(tm < 32, z, 3 - z) + jnp.where(tile < 4, 0, 1)


def place(block, tile):
    low = table([at[0] for at in PLACES], block)
    return tile + jnp.where(tile < 4, low, table([at[1] for at in PLACES], block))


def table(values, at):
    out = values[0]
    for i in range(1, len(values)):
        out = jnp.where(at >= i, values[i], out)
    return out


def kernel(
    x_ref, o_ref, wrapped, gathered, u, v, fine, deltas_own, deltas, s, c, out_rows,
    slab_send, slab_recv, spread_send, delta_recv, state_recv, ends_send, ends_recv, load_sem,
):
    n, sp = lax.axis_index("tm"), lax.axis_index("space")
    tile = tile_of(sp, n)
    block = sum((n >= start).astype(jnp.int32) for start in STARTS[1:BLOCKS])
    left = table(STARTS[1:], block) - 1 - n
    hub = place(block, tile)
    carries = [n == place(b, tile) for b in range(BLOCKS)]
    is_chain = functools.reduce(jnp.logical_or, carries)
    role = sum(b * carries[b].astype(jnp.int32) for b in range(BLOCKS))
    size, first_slice = table(SIZES, role), table(STARTS, role)
    in_own = jnp.logical_and(n >= first_slice, n < first_slice + size)

    loads = [
        pltpu.make_async_copy(
            x_ref.at[0, :, pl.ds(at, rows)], wrapped.at[:, pl.ds(to, rows)], load_sem.at[i]
        )
        for i, (at, rows, to) in enumerate(
            ((0, 96, FSTEPS), (96 - FSTEPS, FSTEPS, 0), (0, FSTEPS, FSTEPS + 96))
        )
    ]
    for cp in loads:
        cp.start()

    barrier = pltpu.get_barrier_semaphore()

    def greet(tm, space):
        pl.semaphore_signal(barrier, inc=1, device_id=(tm, space), device_id_type=MESH)

    for j in range(1, 8):
        greet(n, (sp + j) % 8)

    @pl.when(hub != n)
    def _():
        greet(hub, sp)

    @pl.when(is_chain)
    def _():
        def spoke(i, _):
            @pl.when(first_slice + i != n)
            def _():
                greet(first_slice + i, sp)

            return 0

        lax.fori_loop(0, size, spoke, 0)

        @pl.when(role > 0)
        def _():
            for off in (-2, -1, 0, 1, 2):
                other = (tile + off) % 8
                before = place(role - 1, other)
                greet(before, space_of(other, before))

    spokes = size - jnp.where(in_own, 1, 0) + jnp.where(role < BLOCKS - 1, 5, 0)
    pl.semaphore_wait(barrier, 7 + jnp.where(hub != n, 1, 0) + jnp.where(is_chain, spokes, 0))

    for cp in loads:
        cp.wait()
    copies = []
    for j in range(1, 8):
        to = (sp + j) % 8
        cp = pltpu.make_async_remote_copy(
            src_ref=wrapped.at[:, pl.ds(TILE * tile_of(to, n), WIDE)],
            dst_ref=gathered.at[pl.ds(2 * sp, 2)],
            send_sem=slab_send.at[j],
            recv_sem=slab_recv.at[j],
            device_id=(n, to),
            device_id_type=MESH,
        )
        cp.start()
        copies.append(cp)
    own = pltpu.make_async_copy(
        wrapped.at[:, pl.ds(TILE * tile, WIDE)], gathered.at[pl.ds(2 * sp, 2)], slab_recv.at[0]
    )
    own.start()
    own.wait()
    for cp in copies:
        cp.wait_recv()

    flat = gathered.reshape(16 * WIDE, 128)
    for y in range(WIDE):
        u[y, 0:8] = flat[pl.ds(y, 8, stride=2 * WIDE), :]
        u[y, 8:16] = flat[pl.ds(WIDE + y, 8, stride=2 * WIDE), :]
    own_rows = slice(FSTEPS, FSTEPS + TILE)
    step(u, v, FSTEPS, FSTEPS + TILE, 0.15, 0.1)
    deltas_own[...] = v[own_rows]
    a, b = u, v
    for i in range(FSTEPS):
        step(a, b, i + 1, WIDE - 1 - i, 0.03, 0.02)
        a, b = b, a
    fine[...] = a[own_rows]
    deltas_own[...] = a[own_rows] - deltas_own[...]

    def spread(src, dst_of, recv, to_block, ghost, sends, act):
        near, far = min(ghost, TILE), max(ghost - TILE, 0)
        parts = [(0, 0, TILE, GHOST)]
        if near:
            parts = [(1, TILE - near, near, GHOST - near), (7, 0, near, GHOST + TILE)] + parts
        if far:
            parts = [(2, TILE - far, far, GHOST - TILE - far), (6, 0, far, GHOST + 2 * TILE)] + parts
        for off, at, rows, to in parts:
            dest = (tile + off) % 8
            tm = place(to_block, dest)
            space = space_of(dest, tm)
            src_part, dst_part = src.at[pl.ds(at, rows)], dst_of.at[pl.ds(to, rows)]
            far_copy = pltpu.make_async_remote_copy(
                src_ref=src_part,
                dst_ref=dst_part,
                send_sem=spread_send.at[sends, off],
                recv_sem=recv,
                device_id=(tm, space),
                device_id_type=MESH,
            )
            if off:
                act(far_copy)
            else:
                mine = tm == n

                @pl.when(jnp.logical_not(mine))
                def _():
                    act(far_copy)

                if act is start:

                    @pl.when(mine)
                    def _():
                        pltpu.make_async_copy(src_part, dst_part, recv).start()

    def start(cp):
        cp.start()

    def finish(cp):
        cp.wait_send()

    def spread_deltas(act):
        for rem in range(GHOST):

            @pl.when(jnp.logical_and(left == rem, n > 0))
            def _():
                spread(deltas_own, deltas.at[rem], delta_recv.at[rem], block, rem, 0, act)

    def spread_first(act):
        @pl.when(n == 0)
        def _():
            spread(fine, c, state_recv, 0, SIZES[0] - 1, 1, act)

    spread_first(start)
    spread_deltas(start)
    spread_first(finish)
    spread_deltas(finish)

    flat_out = out_rows.reshape(GHOST * 16 * 16, 128)

    @pl.when(is_chain)
    def _():
        for b in range(BLOCKS):

            @pl.when(role == b)
            def _():
                whole = s.at[pl.ds(0, TILE + 2 * (SIZES[b] if b else SIZES[0] - 1))]
                pltpu.make_async_copy(whole, whole, state_recv).wait()

        def keep_for(rem):
            def keep(y, h, out):
                if GHOST <= y < GHOST + TILE:
                    flat_out[pl.ds(rem * 256 + 16 * h + y - GHOST, 8, stride=32), :] = out

            return keep

        for rem in reversed(range(GHOST)):
            src, dst = (s, c) if rem % 2 else (c, s)
            runs = rem < size
            if rem == SIZES[0] - 1:
                runs = jnp.logical_and(runs, role > 0)

                @pl.when(role == 0)
                def _(rem=rem):
                    for y in range(GHOST, GHOST + TILE):
                        for h in range(2):
                            keep_for(rem)(y, h, c[y, 8 * h : 8 * h + 8])

            @pl.when(runs)
            def _(rem=rem, src=src, dst=dst):
                whole = deltas.at[rem, pl.ds(0, TILE + 2 * rem)]
                pltpu.make_async_copy(whole, whole, delta_recv.at[rem]).wait()
                step(
                    src, dst, GHOST - rem, GHOST + TILE + rem, 0.15, 0.1,
                    lambda y, h: deltas[rem, y, h], keep_for(rem),
                )

        mid = s.at[pl.ds(GHOST, TILE)]

        def pass_on(act):
            for b in range(BLOCKS - 1):

                @pl.when(role == b)
                def _():
                    spread(mid, s, state_recv, b + 1, SIZES[b + 1], 1, act)

        pass_on(start)

        def send(i, _):
            away = 4 + (i + 1) // 2 * (1 - 2 * (i % 2))
            for at in range(2):
                tm = (first_slice // 8 + at) * 8 + (n + away) % 8
                rem = first_slice + size - 1 - tm

                @pl.when(jnp.logical_and(rem >= 0, rem < size))
                def _():
                    for off in range(8):
                        to = (sp + off) % 8
                        src = out_rows.at[pl.ds(16 * rem + 2 * to, 2), pl.ds(0, TILE)]
                        dst = o_ref.at[0, :, pl.ds(TILE * tile, TILE)]
                        remote = pltpu.make_async_remote_copy(
                            src_ref=src,
                            dst_ref=dst,
                            send_sem=ends_send,
                            recv_sem=ends_recv,
                            device_id=(tm, to),
                            device_id_type=MESH,
                        )
                        if off:
                            remote.start()
                        else:

                            @pl.when(tm == n)
                            def _():
                                pltpu.make_async_copy(src, dst, ends_recv).start()

                            @pl.when(tm != n)
                            def _():
                                remote.start()

            return 0

        lax.fori_loop(0, 8, send, 0)
        pass_on(finish)
        for b in range(BLOCKS):

            for own in range(2):

                @pl.when(jnp.logical_and(role == b, in_own == bool(own)))
                def _():
                    count = 8 * SIZES[b] - own
                    sent = out_rows.at[pl.ds(0, 2 * count), pl.ds(0, TILE)]
                    pltpu.make_async_copy(sent, sent, ends_send).wait()

    for cp in copies:
        cp.wait_send()
    pltpu.make_async_copy(o_ref, o_ref, ends_recv).wait()


def per_device(starts):
    field = jnp.float32
    dma = pltpu.SemaphoreType.DMA
    return pl.pallas_call(
        kernel,
        out_shape=jax.ShapeDtypeStruct(starts.shape, starts.dtype),
        in_specs=[pl.BlockSpec(memory_space=pl.ANY)],
        out_specs=pl.BlockSpec(memory_space=pl.ANY),
        scratch_shapes=[
            pltpu.VMEM((2, 96 + 2 * FSTEPS, 128), field),
            pltpu.VMEM((16, WIDE, 128), field),
            pltpu.VMEM((WIDE, 16, 128), field),
            pltpu.VMEM((WIDE, 16, 128), field),
            pltpu.VMEM((TILE, 16, 128), field),
            pltpu.VMEM((TILE, 16, 128), field),
            pltpu.VMEM((GHOST, SPAN, 16, 128), field),
            pltpu.VMEM((SPAN, 16, 128), field),
            pltpu.VMEM((SPAN, 16, 128), field),
            pltpu.VMEM((GHOST * 16, 16, 128), field),
            dma((8,)),
            dma((8,)),
            dma((2, 8)),
            dma((GHOST,)),
            dma,
            dma,
            dma,
            dma((3,)),
        ],
        compiler_params=pltpu.CompilerParams(
            collective_id=0, has_side_effects=True, vmem_limit_bytes=40 << 20
        ),
    )(starts)


def solution(mesh):
    placed = P("tm", "space", None, None)
    return jax.shard_map(
        per_device, mesh=mesh, in_specs=(placed,), out_specs=placed, check_vma=False
    )
```

```python
import functools

import jax
import jax.numpy as jnp
from jax import lax
from jax.experimental import pallas as pl
from jax.experimental.pallas import tpu as pltpu
from jax.sharding import PartitionSpec as P

MESH = pl.DeviceIdType.MESH
FSTEPS = 10
STARTS = (0, 8, 20, 32, 48, 64)
BLOCKS = len(STARTS) - 1
SIZES = tuple(STARTS[b + 1] - STARTS[b] for b in range(BLOCKS))
GHOST = max(SIZES)
SPREAD = max((STARTS[b + 1] - 1) // 8 - STARTS[b] // 8 + 1 for b in range(BLOCKS))
CUTS = sorted({0, 4, SIZES[0] - 1, *SIZES})
PLACES = ((0, 0), (8, 8), (24, 24), (32, 40), (56, 48))
TILE = 12
WIDE = TILE + 2 * FSTEPS
SPAN = TILE + 2 * GHOST


def step(src, dst, first, last, rate, react, more=None, keep=None):
    stay = 1.0 - 6.0 * rate + react
    halves = (slice(0, 8), slice(8, 16))
    below = [src[first - 1, h] for h in halves]
    here = [src[first, h] for h in halves]
    for y in range(first, last):
        above = [src[y + 1, h] for h in halves]
        for h, turn in ((0, 1), (1, 7)):
            v, other = here[h], here[1 - h]
            beside = (
                (other + pltpu.roll(other, turn, 0))
                + (below[h] + above[h])
                + (pltpu.roll(v, 1, 1) + pltpu.roll(v, 127, 1))
            )
            out = v * (stay - react * (v * v)) + rate * beside
            if more is not None:
                out = out + more(y, halves[h])
            dst[y, halves[h]] = out
            if keep is not None:
                keep(y, h, out)
        below, here = here, above


def tile_of(sp, tm):
    z = jnp.where(tm < 32, sp // 2, 3 - sp // 2)
    return jnp.where(sp % 2 == 0, z, 7 - z)


def space_of(tile, tm):
    z = jnp.where(tile < 4, tile, 7 - tile)
    return 2 * jnp.where(tm < 32, z, 3 - z) + jnp.where(tile < 4, 0, 1)


def place(block, tile):
    low = table([at[0] for at in PLACES], block)
    return tile + jnp.where(tile < 4, low, table([at[1] for at in PLACES], block))


def table(values, at):
    out = values[0]
    for i in range(1, len(values)):
        out = jnp.where(at >= i, values[i], out)
    return out


def kernel(
    x_ref, o_ref, wrapped, gathered, u, v, fine, deltas_own, deltas, s, c, out_rows,
    slab_send, slab_recv, spread_send, delta_recv, state_recv, ends_send, ends_recv, load_sem,
):
    n, sp = lax.axis_index("tm"), lax.axis_index("space")
    tile = tile_of(sp, n)
    block = sum((n >= start).astype(jnp.int32) for start in STARTS[1:BLOCKS])
    left = table(STARTS[1:], block) - 1 - n
    hub = place(block, tile)
    carries = [n == place(b, tile) for b in range(BLOCKS)]
    is_chain = functools.reduce(jnp.logical_or, carries)
    role = sum(b * carries[b].astype(jnp.int32) for b in range(BLOCKS))
    size, first_slice = table(SIZES, role), table(STARTS, role)
    in_own = jnp.logical_and(n >= first_slice, n < first_slice + size)

    loads = [
        pltpu.make_async_copy(
            x_ref.at[0, :, pl.ds(at, rows)], wrapped.at[:, pl.ds(to, rows)], load_sem.at[i]
        )
        for i, (at, rows, to) in enumerate(
            ((0, 96, FSTEPS), (96 - FSTEPS, FSTEPS, 0), (0, FSTEPS, FSTEPS + 96))
        )
    ]
    for cp in loads:
        cp.start()

    barrier = pltpu.get_barrier_semaphore()

    def greet(tm, space):
        pl.semaphore_signal(barrier, inc=1, device_id=(tm, space), device_id_type=MESH)

    for j in range(1, 8):
        greet(n, (sp + j) % 8)

    @pl.when(hub != n)
    def _():
        greet(hub, sp)

    @pl.when(is_chain)
    def _():
        def spoke(i, _):
            @pl.when(first_slice + i != n)
            def _():
                greet(first_slice + i, sp)

            return 0

        lax.fori_loop(0, size, spoke, 0)

        @pl.when(role > 0)
        def _():
            for off in (-2, -1, 0, 1, 2):
                other = (tile + off) % 8
                before = place(role - 1, other)
                greet(before, space_of(other, before))

    spokes = size - jnp.where(in_own, 1, 0) + jnp.where(role < BLOCKS - 1, 5, 0)
    pl.semaphore_wait(barrier, 7 + jnp.where(hub != n, 1, 0) + jnp.where(is_chain, spokes, 0))

    for cp in loads:
        cp.wait()
    copies = []
    for j in range(1, 8):
        to = (sp + j) % 8
        cp = pltpu.make_async_remote_copy(
            src_ref=wrapped.at[:, pl.ds(TILE * tile_of(to, n), WIDE)],
            dst_ref=gathered.at[pl.ds(2 * sp, 2)],
            send_sem=slab_send.at[j],
            recv_sem=slab_recv.at[j],
            device_id=(n, to),
            device_id_type=MESH,
        )
        cp.start()
        copies.append(cp)
    own = pltpu.make_async_copy(
        wrapped.at[:, pl.ds(TILE * tile, WIDE)], gathered.at[pl.ds(2 * sp, 2)], slab_recv.at[0]
    )
    own.start()
    own.wait()
    for cp in copies:
        cp.wait_recv()

    flat = gathered.reshape(18 * WIDE, 128)
    for y in range(WIDE):
        u[y, 0:8] = flat[pl.ds(y, 8, stride=2 * WIDE), :]
        u[y, 8:16] = flat[pl.ds(WIDE + y, 8, stride=2 * WIDE), :]
    own_rows = slice(FSTEPS, FSTEPS + TILE)
    step(u, v, FSTEPS, FSTEPS + TILE, 0.15, 0.1)
    deltas_own[...] = v[own_rows]
    a, b = u, v
    for i in range(FSTEPS):
        step(a, b, i + 1, WIDE - 1 - i, 0.03, 0.02)
        a, b = b, a
    fine[...] = a[own_rows]
    deltas_own[...] = a[own_rows] - deltas_own[...]

    def spread(src, dst_of, recv, to_block, ghost, sends, act):
        near, far = min(ghost, TILE), max(ghost - TILE, 0)
        parts = [(0, 0, TILE, GHOST)]
        if near:
            parts = [(1, TILE - near, near, GHOST - near), (7, 0, near, GHOST + TILE)] + parts
        if far:
            parts = [(2, TILE - far, far, GHOST - TILE - far), (6, 0, far, GHOST + 2 * TILE)] + parts
        for off, at, rows, to in parts:
            dest = (tile + off) % 8
            tm = place(to_block, dest)
            space = space_of(dest, tm)
            src_part, dst_part = src.at[pl.ds(at, rows)], dst_of.at[pl.ds(to, rows)]
            far_copy = pltpu.make_async_remote_copy(
                src_ref=src_part,
                dst_ref=dst_part,
                send_sem=spread_send.at[sends, off],
                recv_sem=recv,
                device_id=(tm, space),
                device_id_type=MESH,
            )
            if off:
                act(far_copy)
            else:
                mine = tm == n

                @pl.when(jnp.logical_not(mine))
                def _():
                    act(far_copy)

                if act is start:

                    @pl.when(mine)
                    def _():
                        pltpu.make_async_copy(src_part, dst_part, recv).start()

    def start(cp):
        cp.start()

    def finish(cp):
        cp.wait_send()

    def spread_deltas(act):
        for rem in range(GHOST):

            @pl.when(jnp.logical_and(left == rem, n > 0))
            def _():
                spread(deltas_own, deltas.at[rem], delta_recv.at[rem], block, rem, 0, act)

    def spread_first(act):
        @pl.when(n == 0)
        def _():
            spread(fine, c, state_recv, 0, SIZES[0] - 1, 1, act)

    spread_first(start)
    spread_deltas(start)
    spread_first(finish)
    spread_deltas(finish)

    flat_out = out_rows.reshape((GHOST * 16 + 2) * 16, 128)

    @pl.when(is_chain)
    def _():
        def send(tm):
            rem = first_slice + size - 1 - tm

            @pl.when(jnp.logical_and(rem >= 0, rem < size))
            def _():
                for off in range(8):
                    to = (sp + off) % 8
                    src = out_rows.at[pl.ds(16 * rem + 2 * to, 2), pl.ds(0, TILE)]
                    dst = o_ref.at[0, :, pl.ds(TILE * tile, TILE)]
                    remote = pltpu.make_async_remote_copy(
                        src_ref=src,
                        dst_ref=dst,
                        send_sem=ends_send,
                        recv_sem=ends_recv,
                        device_id=(tm, to),
                        device_id_type=MESH,
                    )
                    if off:
                        remote.start()
                    else:

                        @pl.when(tm == n)
                        def _():
                            pltpu.make_async_copy(src, dst, ends_recv).start()

                        @pl.when(tm != n)
                        def _():
                            remote.start()

        for rem in reversed(range(GHOST)):

            @pl.when(rem < size - jnp.where(role == 0, 1, 0))
            def _(rem=rem):
                whole = deltas.at[rem, pl.ds(0, TILE + 2 * rem)]
                pltpu.make_async_copy(whole, whole, delta_recv.at[rem]).wait()

        for b in range(BLOCKS):

            @pl.when(role == b)
            def _():
                whole = s.at[pl.ds(0, TILE + 2 * (SIZES[b] if b else SIZES[0] - 1))]
                pltpu.make_async_copy(whole, whole, state_recv).wait()

        def keep_for(rem):
            def keep(y, h, out):
                if GHOST <= y < GHOST + TILE:
                    flat_out[pl.ds(rem * 256 + 16 * h + y - GHOST, 8, stride=32), :] = out

            return keep

        @pl.when(role == 0)
        def _():
            for y in range(GHOST, GHOST + TILE):
                for h in range(2):
                    keep_for(SIZES[0] - 1)(y, h, c[y, 8 * h : 8 * h + 8])

        for low, high in reversed(list(zip(CUTS, CUTS[1:]))):

            @pl.when(high <= size - jnp.where(role == 0, 1, 0))
            def _(low=low, high=high):
                for rem in reversed(range(low, high)):
                    src, dst = (s, c) if rem % 2 else (c, s)
                    step(
                        src, dst, GHOST - rem, GHOST + TILE + rem, 0.15, 0.1,
                        lambda y, h, rem=rem: deltas[rem, y, h], keep_for(rem),
                    )

                @pl.when(role == BLOCKS - 1)
                def _():
                    def stretch(i, _):
                        send(first_slice + size - high + i)
                        return 0

                    lax.fori_loop(0, high - low, stretch, 0)

        mid = s.at[pl.ds(GHOST, TILE)]

        def pass_on(act):
            for b in range(BLOCKS - 1):

                @pl.when(role == b)
                def _():
                    spread(mid, s, state_recv, b + 1, SIZES[b + 1], 1, act)

        pass_on(start)

        @pl.when(role < BLOCKS - 1)
        def _():
            def around(i, _):
                away = 4 + (i + 1) // 2 * (1 - 2 * (i % 2))
                for at in range(SPREAD):
                    send((first_slice // 8 + at) * 8 + (n + away) % 8)
                return 0

            lax.fori_loop(0, 8, around, 0)

        pass_on(finish)
        for b in range(BLOCKS):

            for own in range(2):

                @pl.when(jnp.logical_and(role == b, in_own == bool(own)))
                def _():
                    count = 8 * SIZES[b] - own
                    sent = out_rows.at[pl.ds(0, 2 * count), pl.ds(0, TILE)]
                    pltpu.make_async_copy(sent, sent, ends_send).wait()

    for cp in copies:
        cp.wait_send()
    pltpu.make_async_copy(o_ref, o_ref, ends_recv).wait()


def per_device(starts):
    field = jnp.float32
    dma = pltpu.SemaphoreType.DMA
    return pl.pallas_call(
        kernel,
        out_shape=jax.ShapeDtypeStruct(starts.shape, starts.dtype),
        in_specs=[pl.BlockSpec(memory_space=pl.ANY)],
        out_specs=pl.BlockSpec(memory_space=pl.ANY),
        scratch_shapes=[
            pltpu.VMEM((2, 96 + 2 * FSTEPS, 128), field),
            pltpu.VMEM((18, WIDE, 128), field),
            pltpu.VMEM((WIDE, 16, 128), field),
            pltpu.VMEM((WIDE, 16, 128), field),
            pltpu.VMEM((TILE, 16, 128), field),
            pltpu.VMEM((TILE, 16, 128), field),
            pltpu.VMEM((GHOST, SPAN, 16, 128), field),
            pltpu.VMEM((SPAN, 16, 128), field),
            pltpu.VMEM((SPAN, 16, 128), field),
            pltpu.VMEM((GHOST * 16 + 2, 16, 128), field),
            dma((8,)),
            dma((8,)),
            dma((2, 8)),
            dma((GHOST,)),
            dma,
            dma,
            dma,
            dma((3,)),
        ],
        compiler_params=pltpu.CompilerParams(
            collective_id=0, has_side_effects=True, vmem_limit_bytes=40 << 20
        ),
    )(starts)


def solution(mesh):
    placed = P("tm", "space", None, None)
    return jax.shard_map(
        per_device, mesh=mesh, in_specs=(placed,), out_specs=placed, check_vma=False
    )
```

```python
import functools

import jax
import jax.numpy as jnp
from jax import lax
from jax.experimental import pallas as pl
from jax.experimental.pallas import tpu as pltpu
from jax.sharding import PartitionSpec as P

MESH = pl.DeviceIdType.MESH
FSTEPS = 10
STARTS = (0, 8, 20, 32, 48, 64)
BLOCKS = len(STARTS) - 1
SIZES = tuple(STARTS[b + 1] - STARTS[b] for b in range(BLOCKS))
GHOST = max(SIZES)
SPREAD = max((STARTS[b + 1] - 1) // 8 - STARTS[b] // 8 + 1 for b in range(BLOCKS))
CUTS = sorted({0, 4, SIZES[0] - 1, *SIZES})
FIRST_ROWS = (0, 1, 2, 3, 7, 6, 5, 4)
PLACES = ((0, 0), (8, 8), (24, 16), (32, 40), (56, 48))
TILE = 12
WIDE = TILE + 2 * FSTEPS
SPAN = TILE + 2 * GHOST


def step(src, dst, first, last, rate, react, more=None, keep=None):
    stay = 1.0 - 6.0 * rate + react
    halves = (slice(0, 8), slice(8, 16))
    below = [src[first - 1, h] for h in halves]
    here = [src[first, h] for h in halves]
    for y in range(first, last):
        above = [src[y + 1, h] for h in halves]
        for h, turn in ((0, 1), (1, 7)):
            v, other = here[h], here[1 - h]
            beside = (
                (other + pltpu.roll(other, turn, 0))
                + (below[h] + above[h])
                + (pltpu.roll(v, 1, 1) + pltpu.roll(v, 127, 1))
            )
            out = v * (stay - react * (v * v)) + rate * beside
            if more is not None:
                out = out + more(y, halves[h])
            dst[y, halves[h]] = out
            if keep is not None:
                keep(y, h, out)
        below, here = here, above


def tile_of(sp, tm):
    z = jnp.where(tm < 32, sp // 2, 3 - sp // 2)
    return jnp.where(sp % 2 == 0, z, 7 - z)


def space_of(tile, tm):
    z = jnp.where(tile < 4, tile, 7 - tile)
    return 2 * jnp.where(tm < 32, z, 3 - z) + jnp.where(tile < 4, 0, 1)


def place(block, tile):
    low = table([at[0] for at in PLACES], block)
    row = jnp.where(block == 0, table(FIRST_ROWS, tile), tile)
    return row + jnp.where(tile < 4, low, table([at[1] for at in PLACES], block))


def table(values, at):
    out = values[0]
    for i in range(1, len(values)):
        out = jnp.where(at >= i, values[i], out)
    return out


def kernel(
    x_ref, o_ref, wrapped, gathered, u, v, fine, deltas_own, deltas, s, c, out_rows,
    slab_send, slab_recv, spread_send, delta_recv, state_recv, ends_send, ends_recv, load_sem,
):
    n, sp = lax.axis_index("tm"), lax.axis_index("space")
    tile = tile_of(sp, n)
    block = sum((n >= start).astype(jnp.int32) for start in STARTS[1:BLOCKS])
    left = table(STARTS[1:], block) - 1 - n
    hub = place(block, tile)
    carries = [n == place(b, tile) for b in range(BLOCKS)]
    is_chain = functools.reduce(jnp.logical_or, carries)
    role = sum(b * carries[b].astype(jnp.int32) for b in range(BLOCKS))
    size, first_slice = table(SIZES, role), table(STARTS, role)
    in_own = jnp.logical_and(n >= first_slice, n < first_slice + size)

    loads = [
        pltpu.make_async_copy(
            x_ref.at[0, :, pl.ds(at, rows)], wrapped.at[:, pl.ds(to, rows)], load_sem.at[i]
        )
        for i, (at, rows, to) in enumerate(
            ((0, 96, FSTEPS), (96 - FSTEPS, FSTEPS, 0), (0, FSTEPS, FSTEPS + 96))
        )
    ]
    for cp in loads:
        cp.start()

    barrier = pltpu.get_barrier_semaphore()

    def greet(tm, space):
        pl.semaphore_signal(barrier, inc=1, device_id=(tm, space), device_id_type=MESH)

    for j in range(1, 8):
        greet(n, (sp + j) % 8)

    @pl.when(hub != n)
    def _():
        greet(hub, sp)

    @pl.when(is_chain)
    def _():
        def spoke(i, _):
            @pl.when(first_slice + i != n)
            def _():
                greet(first_slice + i, sp)

            return 0

        lax.fori_loop(0, size, spoke, 0)

        @pl.when(role > 0)
        def _():
            for off in (-2, -1, 0, 1, 2):
                other = (tile + off) % 8
                before = place(role - 1, other)
                greet(before, space_of(other, before))

    spokes = size - jnp.where(in_own, 1, 0) + jnp.where(role < BLOCKS - 1, 5, 0)
    pl.semaphore_wait(barrier, 7 + jnp.where(hub != n, 1, 0) + jnp.where(is_chain, spokes, 0))

    for cp in loads:
        cp.wait()
    copies = []
    for j in range(1, 8):
        to = (sp + j) % 8
        cp = pltpu.make_async_remote_copy(
            src_ref=wrapped.at[:, pl.ds(TILE * tile_of(to, n), WIDE)],
            dst_ref=gathered.at[pl.ds(2 * sp, 2)],
            send_sem=slab_send.at[j],
            recv_sem=slab_recv.at[j],
            device_id=(n, to),
            device_id_type=MESH,
        )
        cp.start()
        copies.append(cp)
    own = pltpu.make_async_copy(
        wrapped.at[:, pl.ds(TILE * tile, WIDE)], gathered.at[pl.ds(2 * sp, 2)], slab_recv.at[0]
    )
    own.start()
    own.wait()
    for cp in copies:
        cp.wait_recv()

    flat = gathered.reshape(18 * WIDE, 128)
    for y in range(WIDE):
        u[y, 0:8] = flat[pl.ds(y, 8, stride=2 * WIDE), :]
        u[y, 8:16] = flat[pl.ds(WIDE + y, 8, stride=2 * WIDE), :]
    own_rows = slice(FSTEPS, FSTEPS + TILE)
    step(u, v, FSTEPS, FSTEPS + TILE, 0.15, 0.1)
    deltas_own[...] = v[own_rows]
    a, b = u, v
    for i in range(FSTEPS):
        step(a, b, i + 1, WIDE - 1 - i, 0.03, 0.02)
        a, b = b, a
    fine[...] = a[own_rows]
    deltas_own[...] = a[own_rows] - deltas_own[...]

    def spread(src, dst_of, recv, to_block, ghost, sends, act):
        near, far = min(ghost, TILE), max(ghost - TILE, 0)
        parts = [(0, 0, TILE, GHOST)]
        if near:
            parts = [(1, TILE - near, near, GHOST - near), (7, 0, near, GHOST + TILE)] + parts
        if far:
            parts = [(2, TILE - far, far, GHOST - TILE - far), (6, 0, far, GHOST + 2 * TILE)] + parts
        for off, at, rows, to in parts:
            dest = (tile + off) % 8
            tm = place(to_block, dest)
            space = space_of(dest, tm)
            src_part, dst_part = src.at[pl.ds(at, rows)], dst_of.at[pl.ds(to, rows)]
            far_copy = pltpu.make_async_remote_copy(
                src_ref=src_part,
                dst_ref=dst_part,
                send_sem=spread_send.at[sends, off],
                recv_sem=recv,
                device_id=(tm, space),
                device_id_type=MESH,
            )
            if off:
                act(far_copy)
            else:
                mine = tm == n

                @pl.when(jnp.logical_not(mine))
                def _():
                    act(far_copy)

                if act is start:

                    @pl.when(mine)
                    def _():
                        pltpu.make_async_copy(src_part, dst_part, recv).start()

    def start(cp):
        cp.start()

    def finish(cp):
        cp.wait_send()

    def spread_deltas(act):
        for rem in range(GHOST):

            @pl.when(jnp.logical_and(left == rem, n > 0))
            def _():
                spread(deltas_own, deltas.at[rem], delta_recv.at[rem], block, rem, 0, act)

    def spread_first(act):
        @pl.when(n == 0)
        def _():
            spread(fine, c, state_recv, 0, SIZES[0] - 1, 1, act)

    spread_first(start)
    spread_deltas(start)
    spread_first(finish)
    spread_deltas(finish)

    flat_out = out_rows.reshape((GHOST * 16 + 2) * 16, 128)

    @pl.when(is_chain)
    def _():
        def send(tm):
            rem = first_slice + size - 1 - tm

            @pl.when(jnp.logical_and(rem >= 0, rem < size))
            def _():
                for off in range(8):
                    to = (sp + off) % 8
                    src = out_rows.at[pl.ds(16 * rem + 2 * to, 2), pl.ds(0, TILE)]
                    dst = o_ref.at[0, :, pl.ds(TILE * tile, TILE)]
                    remote = pltpu.make_async_remote_copy(
                        src_ref=src,
                        dst_ref=dst,
                        send_sem=ends_send,
                        recv_sem=ends_recv,
                        device_id=(tm, to),
                        device_id_type=MESH,
                    )
                    if off:
                        remote.start()
                    else:

                        @pl.when(tm == n)
                        def _():
                            pltpu.make_async_copy(src, dst, ends_recv).start()

                        @pl.when(tm != n)
                        def _():
                            remote.start()

        for rem in reversed(range(GHOST)):

            @pl.when(rem < size - jnp.where(role == 0, 1, 0))
            def _(rem=rem):
                whole = deltas.at[rem, pl.ds(0, TILE + 2 * rem)]
                pltpu.make_async_copy(whole, whole, delta_recv.at[rem]).wait()

        for b in range(BLOCKS):

            @pl.when(role == b)
            def _():
                whole = s.at[pl.ds(0, TILE + 2 * (SIZES[b] if b else SIZES[0] - 1))]
                pltpu.make_async_copy(whole, whole, state_recv).wait()

        def keep_for(rem):
            def keep(y, h, out):
                if GHOST <= y < GHOST + TILE:
                    flat_out[pl.ds(rem * 256 + 16 * h + y - GHOST, 8, stride=32), :] = out

            return keep

        @pl.when(role == 0)
        def _():
            for y in range(GHOST, GHOST + TILE):
                for h in range(2):
                    keep_for(SIZES[0] - 1)(y, h, c[y, 8 * h : 8 * h + 8])

        for low, high in reversed(list(zip(CUTS, CUTS[1:]))):

            @pl.when(high <= size - jnp.where(role == 0, 1, 0))
            def _(low=low, high=high):
                for rem in reversed(range(low, high)):
                    src, dst = (s, c) if rem % 2 else (c, s)
                    step(
                        src, dst, GHOST - rem, GHOST + TILE + rem, 0.15, 0.1,
                        lambda y, h, rem=rem: deltas[rem, y, h], keep_for(rem),
                    )

                @pl.when(role == BLOCKS - 1)
                def _():
                    def stretch(i, _):
                        send(first_slice + size - high + i)
                        return 0

                    lax.fori_loop(0, high - low, stretch, 0)

        mid = s.at[pl.ds(GHOST, TILE)]

        def pass_on(act):
            for b in range(BLOCKS - 1):

                @pl.when(role == b)
                def _():
                    spread(mid, s, state_recv, b + 1, SIZES[b + 1], 1, act)

        pass_on(start)

        @pl.when(role < BLOCKS - 1)
        def _():
            def around(i, _):
                away = 4 + (i + 1) // 2 * (1 - 2 * (i % 2))
                for at in range(SPREAD):
                    send((first_slice // 8 + at) * 8 + (n + away) % 8)
                return 0

            lax.fori_loop(0, 8, around, 0)

        pass_on(finish)
        for b in range(BLOCKS):

            for own in range(2):

                @pl.when(jnp.logical_and(role == b, in_own == bool(own)))
                def _():
                    count = 8 * SIZES[b] - own
                    sent = out_rows.at[pl.ds(0, 2 * count), pl.ds(0, TILE)]
                    pltpu.make_async_copy(sent, sent, ends_send).wait()

    for cp in copies:
        cp.wait_send()
    pltpu.make_async_copy(o_ref, o_ref, ends_recv).wait()


def per_device(starts):
    field = jnp.float32
    dma = pltpu.SemaphoreType.DMA
    return pl.pallas_call(
        kernel,
        out_shape=jax.ShapeDtypeStruct(starts.shape, starts.dtype),
        in_specs=[pl.BlockSpec(memory_space=pl.ANY)],
        out_specs=pl.BlockSpec(memory_space=pl.ANY),
        scratch_shapes=[
            pltpu.VMEM((2, 96 + 2 * FSTEPS, 128), field),
            pltpu.VMEM((18, WIDE, 128), field),
            pltpu.VMEM((WIDE, 16, 128), field),
            pltpu.VMEM((WIDE, 16, 128), field),
            pltpu.VMEM((TILE, 16, 128), field),
            pltpu.VMEM((TILE, 16, 128), field),
            pltpu.VMEM((GHOST, SPAN, 16, 128), field),
            pltpu.VMEM((SPAN, 16, 128), field),
            pltpu.VMEM((SPAN, 16, 128), field),
            pltpu.VMEM((GHOST * 16 + 2, 16, 128), field),
            dma((8,)),
            dma((8,)),
            dma((2, 8)),
            dma((GHOST,)),
            dma,
            dma,
            dma,
            dma((3,)),
        ],
        compiler_params=pltpu.CompilerParams(
            collective_id=0, has_side_effects=True, vmem_limit_bytes=40 << 20
        ),
    )(starts)


def solution(mesh):
    placed = P("tm", "space", None, None)
    return jax.shard_map(
        per_device, mesh=mesh, in_specs=(placed,), out_specs=placed, check_vma=False
    )
```

```python
import functools

import jax
import jax.numpy as jnp
from jax import lax
from jax.experimental import pallas as pl
from jax.experimental.pallas import tpu as pltpu
from jax.sharding import PartitionSpec as P

MESH = pl.DeviceIdType.MESH
FSTEPS = 10
STARTS = (0, 8, 20, 32, 48, 64)
BLOCKS = len(STARTS) - 1
SIZES = tuple(STARTS[b + 1] - STARTS[b] for b in range(BLOCKS))
GHOST = max(SIZES)
SPREAD = max((STARTS[b + 1] - 1) // 8 - STARTS[b] // 8 + 1 for b in range(BLOCKS))
CUTS = sorted({0, 2, 4, SIZES[0] - 1, *SIZES})
FIRST_ROWS = (1, 1, 2, 2, 6, 6, 5, 5)
PLACES = ((0, 0), (8, 8), (24, 16), (32, 40), (56, 48))
TILE = 12
WIDE = TILE + 2 * FSTEPS
SPAN = TILE + 2 * GHOST


def step(src, dst, first, last, rate, react, more=None, keep=None):
    stay = 1.0 - 6.0 * rate + react
    halves = (slice(0, 8), slice(8, 16))
    below = [src[first - 1, h] for h in halves]
    here = [src[first, h] for h in halves]
    for y in range(first, last):
        above = [src[y + 1, h] for h in halves]
        for h, turn in ((0, 1), (1, 7)):
            v, other = here[h], here[1 - h]
            beside = (
                (other + pltpu.roll(other, turn, 0))
                + (below[h] + above[h])
                + (pltpu.roll(v, 1, 1) + pltpu.roll(v, 127, 1))
            )
            out = v * (stay - react * (v * v)) + rate * beside
            if more is not None:
                out = out + more(y, halves[h])
            dst[y, halves[h]] = out
            if keep is not None:
                keep(y, h, out)
        below, here = here, above


def tile_of(sp, tm):
    z = jnp.where(tm < 32, sp // 2, 3 - sp // 2)
    return jnp.where(sp % 2 == 0, z, 7 - z)


def space_of(tile, tm):
    z = jnp.where(tile < 4, tile, 7 - tile)
    return 2 * jnp.where(tm < 32, z, 3 - z) + jnp.where(tile < 4, 0, 1)


def place(block, tile):
    low = table([at[0] for at in PLACES], block)
    row = jnp.where(block == 0, table(FIRST_ROWS, tile), tile)
    return row + jnp.where(tile < 4, low, table([at[1] for at in PLACES], block))


def table(values, at):
    out = values[0]
    for i in range(1, len(values)):
        out = jnp.where(at >= i, values[i], out)
    return out


def kernel(
    x_ref, o_ref, wrapped, gathered, u, v, fine, deltas_own, deltas, s, c, out_rows,
    slab_send, slab_recv, spread_send, delta_recv, state_recv, ends_send, ends_recv, load_sem,
):
    n, sp = lax.axis_index("tm"), lax.axis_index("space")
    tile = tile_of(sp, n)
    block = sum((n >= start).astype(jnp.int32) for start in STARTS[1:BLOCKS])
    left = table(STARTS[1:], block) - 1 - n
    hub = place(block, tile)
    carries = [n == place(b, tile) for b in range(BLOCKS)]
    is_chain = functools.reduce(jnp.logical_or, carries)
    role = sum(b * carries[b].astype(jnp.int32) for b in range(BLOCKS))
    size, first_slice = table(SIZES, role), table(STARTS, role)
    in_own = jnp.logical_and(n >= first_slice, n < first_slice + size)

    loads = [
        pltpu.make_async_copy(
            x_ref.at[0, :, pl.ds(at, rows)], wrapped.at[:, pl.ds(to, rows)], load_sem.at[i]
        )
        for i, (at, rows, to) in enumerate(
            ((0, 96, FSTEPS), (96 - FSTEPS, FSTEPS, 0), (0, FSTEPS, FSTEPS + 96))
        )
    ]
    for cp in loads:
        cp.start()

    barrier = pltpu.get_barrier_semaphore()

    def greet(tm, space):
        pl.semaphore_signal(barrier, inc=1, device_id=(tm, space), device_id_type=MESH)

    for j in range(1, 8):
        greet(n, (sp + j) % 8)

    @pl.when(hub != n)
    def _():
        greet(hub, sp)

    @pl.when(is_chain)
    def _():
        def spoke(i, _):
            @pl.when(first_slice + i != n)
            def _():
                greet(first_slice + i, sp)

            return 0

        lax.fori_loop(0, size, spoke, 0)

        @pl.when(role > 0)
        def _():
            for off in (-2, -1, 0, 1, 2):
                other = (tile + off) % 8
                before = place(role - 1, other)
                greet(before, space_of(other, before))

    spokes = size - jnp.where(in_own, 1, 0) + jnp.where(role < BLOCKS - 1, 5, 0)
    pl.semaphore_wait(barrier, 7 + jnp.where(hub != n, 1, 0) + jnp.where(is_chain, spokes, 0))

    for cp in loads:
        cp.wait()
    copies = []
    for j, (dz, flip) in enumerate(((2, 0), (2, 1), (3, 0), (3, 1), (1, 0), (1, 1), (0, 1)), 1):
        to = (sp // 2 + dz) % 4 * 2 + (sp + flip) % 2
        cp = pltpu.make_async_remote_copy(
            src_ref=wrapped.at[:, pl.ds(TILE * tile_of(to, n), WIDE)],
            dst_ref=gathered.at[pl.ds(2 * sp, 2)],
            send_sem=slab_send.at[j],
            recv_sem=slab_recv.at[j],
            device_id=(n, to),
            device_id_type=MESH,
        )
        cp.start()
        copies.append(cp)
    own = pltpu.make_async_copy(
        wrapped.at[:, pl.ds(TILE * tile, WIDE)], gathered.at[pl.ds(2 * sp, 2)], slab_recv.at[0]
    )
    own.start()
    own.wait()
    for cp in copies:
        cp.wait_recv()

    flat = gathered.reshape(18 * WIDE, 128)
    for y in range(WIDE):
        u[y, 0:8] = flat[pl.ds(y, 8, stride=2 * WIDE), :]
        u[y, 8:16] = flat[pl.ds(WIDE + y, 8, stride=2 * WIDE), :]
    own_rows = slice(FSTEPS, FSTEPS + TILE)
    step(u, v, FSTEPS, FSTEPS + TILE, 0.15, 0.1)
    deltas_own[...] = v[own_rows]
    a, b = u, v
    for i in range(FSTEPS):
        step(a, b, i + 1, WIDE - 1 - i, 0.03, 0.02)
        a, b = b, a
    fine[...] = a[own_rows]
    deltas_own[...] = a[own_rows] - deltas_own[...]

    def spread(src, dst_of, recv, to_block, ghost, sends, act):
        near, far = min(ghost, TILE), max(ghost - TILE, 0)
        parts = [(0, 0, TILE, GHOST)]
        if near:
            parts = [(1, TILE - near, near, GHOST - near), (7, 0, near, GHOST + TILE)] + parts
        if far:
            parts = [(2, TILE - far, far, GHOST - TILE - far), (6, 0, far, GHOST + 2 * TILE)] + parts
        for off, at, rows, to in parts:
            dest = (tile + off) % 8
            tm = place(to_block, dest)
            space = space_of(dest, tm)
            src_part, dst_part = src.at[pl.ds(at, rows)], dst_of.at[pl.ds(to, rows)]
            far_copy = pltpu.make_async_remote_copy(
                src_ref=src_part,
                dst_ref=dst_part,
                send_sem=spread_send.at[sends, off],
                recv_sem=recv,
                device_id=(tm, space),
                device_id_type=MESH,
            )
            if off:
                act(far_copy)
            else:
                mine = tm == n

                @pl.when(jnp.logical_not(mine))
                def _():
                    act(far_copy)

                if act is start:

                    @pl.when(mine)
                    def _():
                        pltpu.make_async_copy(src_part, dst_part, recv).start()

    def start(cp):
        cp.start()

    def finish(cp):
        cp.wait_send()

    def spread_deltas(act):
        for rem in range(GHOST):

            @pl.when(jnp.logical_and(left == rem, n > 0))
            def _():
                spread(deltas_own, deltas.at[rem], delta_recv.at[rem], block, rem, 0, act)

    def spread_first(act):
        @pl.when(n == 0)
        def _():
            spread(fine, c, state_recv, 0, SIZES[0] - 1, 1, act)

    spread_first(start)
    spread_deltas(start)
    spread_first(finish)
    spread_deltas(finish)

    flat_out = out_rows.reshape((GHOST * 16 + 2) * 16, 128)

    @pl.when(is_chain)
    def _():
        def send(tm):
            rem = first_slice + size - 1 - tm

            @pl.when(jnp.logical_and(rem >= 0, rem < size))
            def _():
                for off in range(8):
                    to = (sp + off) % 8
                    src = out_rows.at[pl.ds(16 * rem + 2 * to, 2), pl.ds(0, TILE)]
                    dst = o_ref.at[0, :, pl.ds(TILE * tile, TILE)]
                    remote = pltpu.make_async_remote_copy(
                        src_ref=src,
                        dst_ref=dst,
                        send_sem=ends_send,
                        recv_sem=ends_recv,
                        device_id=(tm, to),
                        device_id_type=MESH,
                    )
                    if off:
                        remote.start()
                    else:

                        @pl.when(tm == n)
                        def _():
                            pltpu.make_async_copy(src, dst, ends_recv).start()

                        @pl.when(tm != n)
                        def _():
                            remote.start()

        for rem in reversed(range(GHOST)):

            @pl.when(rem < size - jnp.where(role == 0, 1, 0))
            def _(rem=rem):
                whole = deltas.at[rem, pl.ds(0, TILE + 2 * rem)]
                pltpu.make_async_copy(whole, whole, delta_recv.at[rem]).wait()

        for b in range(BLOCKS):

            @pl.when(role == b)
            def _():
                whole = s.at[pl.ds(0, TILE + 2 * (SIZES[b] if b else SIZES[0] - 1))]
                pltpu.make_async_copy(whole, whole, state_recv).wait()

        def keep_for(rem):
            def keep(y, h, out):
                if GHOST <= y < GHOST + TILE:
                    flat_out[pl.ds(rem * 256 + 16 * h + y - GHOST, 8, stride=32), :] = out

            return keep

        @pl.when(role == 0)
        def _():
            for y in range(GHOST, GHOST + TILE):
                for h in range(2):
                    keep_for(SIZES[0] - 1)(y, h, c[y, 8 * h : 8 * h + 8])

        for low, high in reversed(list(zip(CUTS, CUTS[1:]))):

            @pl.when(high <= size - jnp.where(role == 0, 1, 0))
            def _(low=low, high=high):
                for rem in reversed(range(low, high)):
                    src, dst = (s, c) if rem % 2 else (c, s)
                    step(
                        src, dst, GHOST - rem, GHOST + TILE + rem, 0.15, 0.1,
                        lambda y, h, rem=rem: deltas[rem, y, h], keep_for(rem),
                    )

                @pl.when(role == BLOCKS - 1)
                def _():
                    def stretch(i, _):
                        send(first_slice + size - high + i)
                        return 0

                    lax.fori_loop(0, high - low, stretch, 0)

        mid = s.at[pl.ds(GHOST, TILE)]

        def pass_on(act):
            for b in range(BLOCKS - 1):

                @pl.when(role == b)
                def _():
                    spread(mid, s, state_recv, b + 1, SIZES[b + 1], 1, act)

        pass_on(start)

        @pl.when(role < BLOCKS - 1)
        def _():
            def around(i, _):
                away = 4 + (i + 1) // 2 * (1 - 2 * (i % 2))
                for at in range(SPREAD):
                    send((first_slice // 8 + at) * 8 + (n + away) % 8)
                return 0

            lax.fori_loop(0, 8, around, 0)

        pass_on(finish)
        for b in range(BLOCKS):

            for own in range(2):

                @pl.when(jnp.logical_and(role == b, in_own == bool(own)))
                def _():
                    count = 8 * SIZES[b] - own
                    sent = out_rows.at[pl.ds(0, 2 * count), pl.ds(0, TILE)]
                    pltpu.make_async_copy(sent, sent, ends_send).wait()

    for cp in copies:
        cp.wait_send()
    pltpu.make_async_copy(o_ref, o_ref, ends_recv).wait()


def per_device(starts):
    field = jnp.float32
    dma = pltpu.SemaphoreType.DMA
    return pl.pallas_call(
        kernel,
        out_shape=jax.ShapeDtypeStruct(starts.shape, starts.dtype),
        in_specs=[pl.BlockSpec(memory_space=pl.ANY)],
        out_specs=pl.BlockSpec(memory_space=pl.ANY),
        scratch_shapes=[
            pltpu.VMEM((2, 96 + 2 * FSTEPS, 128), field),
            pltpu.VMEM((18, WIDE, 128), field),
            pltpu.VMEM((WIDE, 16, 128), field),
            pltpu.VMEM((WIDE, 16, 128), field),
            pltpu.VMEM((TILE, 16, 128), field),
            pltpu.VMEM((TILE, 16, 128), field),
            pltpu.VMEM((GHOST, SPAN, 16, 128), field),
            pltpu.VMEM((SPAN, 16, 128), field),
            pltpu.VMEM((SPAN, 16, 128), field),
            pltpu.VMEM((GHOST * 16 + 2, 16, 128), field),
            dma((8,)),
            dma((8,)),
            dma((2, 8)),
            dma((GHOST,)),
            dma,
            dma,
            dma,
            dma((3,)),
        ],
        compiler_params=pltpu.CompilerParams(
            collective_id=0, has_side_effects=True, vmem_limit_bytes=40 << 20
        ),
    )(starts)


def solution(mesh):
    placed = P("tm", "space", None, None)
    return jax.shard_map(
        per_device, mesh=mesh, in_specs=(placed,), out_specs=placed, check_vma=False
    )
```

```python
import functools

import jax
import jax.numpy as jnp
from jax import lax
from jax.experimental import pallas as pl
from jax.experimental.pallas import tpu as pltpu
from jax.sharding import PartitionSpec as P

MESH = pl.DeviceIdType.MESH
FSTEPS = 10
STARTS = (0, 8, 20, 32, 48, 64)
BLOCKS = len(STARTS) - 1
SIZES = tuple(STARTS[b + 1] - STARTS[b] for b in range(BLOCKS))
GHOST = max(SIZES)
SPREAD = max((STARTS[b + 1] - 1) // 8 - STARTS[b] // 8 + 1 for b in range(BLOCKS))
CUTS = sorted({0, 2, 4, SIZES[0] - 1, *SIZES})
FIRST_ROWS = (1, 1, 2, 2, 6, 6, 5, 5)
PLACES = ((0, 0), (8, 8), (24, 16), (32, 40), (56, 48))
SCALE = (2.0 / 3.0) ** 0.5
TILE = 12
WIDE = TILE + 2 * FSTEPS
SPAN = TILE + 2 * GHOST


def step(src, dst, first, last, rate, react, more=None, keep=None):
    stay = (1.0 - 6.0 * rate + react) / rate
    halves = (slice(0, 8), slice(8, 16))
    below = [src[first - 1, h] for h in halves]
    here = [src[first, h] for h in halves]
    for y in range(first, last):
        above = [src[y + 1, h] for h in halves]
        for h, turn in ((0, 1), (1, 7)):
            v, other = here[h], here[1 - h]
            beside = (
                (other + pltpu.roll(other, turn, 0))
                + (below[h] + above[h])
                + (pltpu.roll(v, 1, 1) + pltpu.roll(v, 127, 1))
            )
            out = rate * (v * (stay - v * v) + beside)
            if more is not None:
                out = out + more(y, halves[h])
            dst[y, halves[h]] = out
            if keep is not None:
                keep(y, h, out)
        below, here = here, above


def tile_of(sp, tm):
    z = jnp.where(tm < 32, sp // 2, 3 - sp // 2)
    return jnp.where(sp % 2 == 0, z, 7 - z)


def space_of(tile, tm):
    z = jnp.where(tile < 4, tile, 7 - tile)
    return 2 * jnp.where(tm < 32, z, 3 - z) + jnp.where(tile < 4, 0, 1)


def place(block, tile):
    low = table([at[0] for at in PLACES], block)
    row = jnp.where(block == 0, table(FIRST_ROWS, tile), tile)
    return row + jnp.where(tile < 4, low, table([at[1] for at in PLACES], block))


def table(values, at):
    out = values[0]
    for i in range(1, len(values)):
        out = jnp.where(at >= i, values[i], out)
    return out


def kernel(
    x_ref, o_ref, wrapped, gathered, u, v, fine, deltas_own, deltas, s, c, out_rows,
    slab_send, slab_recv, spread_send, delta_recv, state_recv, ends_send, ends_recv, load_sem,
):
    n, sp = lax.axis_index("tm"), lax.axis_index("space")
    tile = tile_of(sp, n)
    block = sum((n >= start).astype(jnp.int32) for start in STARTS[1:BLOCKS])
    left = table(STARTS[1:], block) - 1 - n
    hub = place(block, tile)
    carries = [n == place(b, tile) for b in range(BLOCKS)]
    is_chain = functools.reduce(jnp.logical_or, carries)
    role = sum(b * carries[b].astype(jnp.int32) for b in range(BLOCKS))
    size, first_slice = table(SIZES, role), table(STARTS, role)
    in_own = jnp.logical_and(n >= first_slice, n < first_slice + size)

    loads = [
        pltpu.make_async_copy(
            x_ref.at[0, :, pl.ds(at, rows)], wrapped.at[:, pl.ds(to, rows)], load_sem.at[i]
        )
        for i, (at, rows, to) in enumerate(
            ((0, 96, FSTEPS), (96 - FSTEPS, FSTEPS, 0), (0, FSTEPS, FSTEPS + 96))
        )
    ]
    for cp in loads:
        cp.start()

    barrier = pltpu.get_barrier_semaphore()

    def greet(tm, space):
        pl.semaphore_signal(barrier, inc=1, device_id=(tm, space), device_id_type=MESH)

    for j in range(1, 8):
        greet(n, (sp + j) % 8)

    @pl.when(hub != n)
    def _():
        greet(hub, sp)

    @pl.when(is_chain)
    def _():
        def spoke(i, _):
            @pl.when(first_slice + i != n)
            def _():
                greet(first_slice + i, sp)

            return 0

        lax.fori_loop(0, size, spoke, 0)

        @pl.when(role > 0)
        def _():
            for off in (-2, -1, 0, 1, 2):
                other = (tile + off) % 8
                before = place(role - 1, other)
                greet(before, space_of(other, before))

    spokes = size - jnp.where(in_own, 1, 0) + jnp.where(role < BLOCKS - 1, 5, 0)
    pl.semaphore_wait(barrier, 7 + jnp.where(hub != n, 1, 0) + jnp.where(is_chain, spokes, 0))

    for cp in loads:
        cp.wait()
    copies = []
    for j, (dz, flip) in enumerate(((2, 0), (2, 1), (3, 0), (3, 1), (1, 0), (1, 1), (0, 1)), 1):
        to = (sp // 2 + dz) % 4 * 2 + (sp + flip) % 2
        cp = pltpu.make_async_remote_copy(
            src_ref=wrapped.at[:, pl.ds(TILE * tile_of(to, n), WIDE)],
            dst_ref=gathered.at[pl.ds(2 * sp, 2)],
            send_sem=slab_send.at[j],
            recv_sem=slab_recv.at[j],
            device_id=(n, to),
            device_id_type=MESH,
        )
        cp.start()
        copies.append(cp)
    own = pltpu.make_async_copy(
        wrapped.at[:, pl.ds(TILE * tile, WIDE)], gathered.at[pl.ds(2 * sp, 2)], slab_recv.at[0]
    )
    own.start()
    own.wait()
    for cp in copies:
        cp.wait_recv()

    flat = gathered.reshape(18 * WIDE, 128)
    for y in range(WIDE):
        u[y, 0:8] = SCALE * flat[pl.ds(y, 8, stride=2 * WIDE), :]
        u[y, 8:16] = SCALE * flat[pl.ds(WIDE + y, 8, stride=2 * WIDE), :]
    own_rows = slice(FSTEPS, FSTEPS + TILE)
    step(u, v, FSTEPS, FSTEPS + TILE, 0.15, 0.1)
    deltas_own[...] = v[own_rows]
    a, b = u, v
    for i in range(FSTEPS):
        step(a, b, i + 1, WIDE - 1 - i, 0.03, 0.02)
        a, b = b, a
    fine[...] = a[own_rows]
    deltas_own[...] = a[own_rows] - deltas_own[...]

    def spread(src, dst_of, recv, to_block, ghost, sends, act):
        near, far = min(ghost, TILE), max(ghost - TILE, 0)
        parts = [(0, 0, TILE, GHOST)]
        if near:
            parts = [(1, TILE - near, near, GHOST - near), (7, 0, near, GHOST + TILE)] + parts
        if far:
            parts = [(2, TILE - far, far, GHOST - TILE - far), (6, 0, far, GHOST + 2 * TILE)] + parts
        for off, at, rows, to in parts:
            dest = (tile + off) % 8
            tm = place(to_block, dest)
            space = space_of(dest, tm)
            src_part, dst_part = src.at[pl.ds(at, rows)], dst_of.at[pl.ds(to, rows)]
            far_copy = pltpu.make_async_remote_copy(
                src_ref=src_part,
                dst_ref=dst_part,
                send_sem=spread_send.at[sends, off],
                recv_sem=recv,
                device_id=(tm, space),
                device_id_type=MESH,
            )
            if off:
                act(far_copy)
            else:
                mine = tm == n

                @pl.when(jnp.logical_not(mine))
                def _():
                    act(far_copy)

                if act is start:

                    @pl.when(mine)
                    def _():
                        pltpu.make_async_copy(src_part, dst_part, recv).start()

    def start(cp):
        cp.start()

    def finish(cp):
        cp.wait_send()

    def spread_deltas(act):
        for rem in range(GHOST):

            @pl.when(jnp.logical_and(left == rem, n > 0))
            def _():
                spread(deltas_own, deltas.at[rem], delta_recv.at[rem], block, rem, 0, act)

    def spread_first(act):
        @pl.when(n == 0)
        def _():
            spread(fine, c, state_recv, 0, SIZES[0] - 1, 1, act)

    spread_first(start)
    spread_deltas(start)
    spread_first(finish)
    spread_deltas(finish)

    flat_out = out_rows.reshape((GHOST * 16 + 2) * 16, 128)

    @pl.when(is_chain)
    def _():
        def send(tm):
            rem = first_slice + size - 1 - tm

            @pl.when(jnp.logical_and(rem >= 0, rem < size))
            def _():
                for off in range(8):
                    to = (sp + off) % 8
                    src = out_rows.at[pl.ds(16 * rem + 2 * to, 2), pl.ds(0, TILE)]
                    dst = o_ref.at[0, :, pl.ds(TILE * tile, TILE)]
                    remote = pltpu.make_async_remote_copy(
                        src_ref=src,
                        dst_ref=dst,
                        send_sem=ends_send,
                        recv_sem=ends_recv,
                        device_id=(tm, to),
                        device_id_type=MESH,
                    )
                    if off:
                        remote.start()
                    else:

                        @pl.when(tm == n)
                        def _():
                            pltpu.make_async_copy(src, dst, ends_recv).start()

                        @pl.when(tm != n)
                        def _():
                            remote.start()

        for rem in reversed(range(GHOST)):

            @pl.when(rem < size - jnp.where(role == 0, 1, 0))
            def _(rem=rem):
                whole = deltas.at[rem, pl.ds(0, TILE + 2 * rem)]
                pltpu.make_async_copy(whole, whole, delta_recv.at[rem]).wait()

        for b in range(BLOCKS):

            @pl.when(role == b)
            def _():
                whole = s.at[pl.ds(0, TILE + 2 * (SIZES[b] if b else SIZES[0] - 1))]
                pltpu.make_async_copy(whole, whole, state_recv).wait()

        def keep_for(rem):
            def keep(y, h, out):
                if GHOST <= y < GHOST + TILE:
                    flat_out[pl.ds(rem * 256 + 16 * h + y - GHOST, 8, stride=32), :] = out * (1.0 / SCALE)

            return keep

        @pl.when(role == 0)
        def _():
            for y in range(GHOST, GHOST + TILE):
                for h in range(2):
                    keep_for(SIZES[0] - 1)(y, h, c[y, 8 * h : 8 * h + 8])

        for low, high in reversed(list(zip(CUTS, CUTS[1:]))):

            @pl.when(high <= size - jnp.where(role == 0, 1, 0))
            def _(low=low, high=high):
                for rem in reversed(range(low, high)):
                    src, dst = (s, c) if rem % 2 else (c, s)
                    step(
                        src, dst, GHOST - rem, GHOST + TILE + rem, 0.15, 0.1,
                        lambda y, h, rem=rem: deltas[rem, y, h], keep_for(rem),
                    )

                @pl.when(role == BLOCKS - 1)
                def _():
                    def stretch(i, _):
                        send(first_slice + size - high + i)
                        return 0

                    lax.fori_loop(0, high - low, stretch, 0)

        mid = s.at[pl.ds(GHOST, TILE)]

        def pass_on(act):
            for b in range(BLOCKS - 1):

                @pl.when(role == b)
                def _():
                    spread(mid, s, state_recv, b + 1, SIZES[b + 1], 1, act)

        pass_on(start)

        @pl.when(role < BLOCKS - 1)
        def _():
            def around(i, _):
                away = 4 + (i + 1) // 2 * (1 - 2 * (i % 2))
                for at in range(SPREAD):
                    send((first_slice // 8 + at) * 8 + (n + away) % 8)
                return 0

            lax.fori_loop(0, 8, around, 0)

        pass_on(finish)
        for b in range(BLOCKS):

            for own in range(2):

                @pl.when(jnp.logical_and(role == b, in_own == bool(own)))
                def _():
                    count = 8 * SIZES[b] - own
                    sent = out_rows.at[pl.ds(0, 2 * count), pl.ds(0, TILE)]
                    pltpu.make_async_copy(sent, sent, ends_send).wait()

    for cp in copies:
        cp.wait_send()
    pltpu.make_async_copy(o_ref, o_ref, ends_recv).wait()


def per_device(starts):
    field = jnp.float32
    dma = pltpu.SemaphoreType.DMA
    return pl.pallas_call(
        kernel,
        out_shape=jax.ShapeDtypeStruct(starts.shape, starts.dtype),
        in_specs=[pl.BlockSpec(memory_space=pl.ANY)],
        out_specs=pl.BlockSpec(memory_space=pl.ANY),
        scratch_shapes=[
            pltpu.VMEM((2, 96 + 2 * FSTEPS, 128), field),
            pltpu.VMEM((18, WIDE, 128), field),
            pltpu.VMEM((WIDE, 16, 128), field),
            pltpu.VMEM((WIDE, 16, 128), field),
            pltpu.VMEM((TILE, 16, 128), field),
            pltpu.VMEM((TILE, 16, 128), field),
            pltpu.VMEM((GHOST, SPAN, 16, 128), field),
            pltpu.VMEM((SPAN, 16, 128), field),
            pltpu.VMEM((SPAN, 16, 128), field),
            pltpu.VMEM((GHOST * 16 + 2, 16, 128), field),
            dma((8,)),
            dma((8,)),
            dma((2, 8)),
            dma((GHOST,)),
            dma,
            dma,
            dma,
            dma((3,)),
        ],
        compiler_params=pltpu.CompilerParams(
            collective_id=0, has_side_effects=True, vmem_limit_bytes=40 << 20
        ),
    )(starts)


def solution(mesh):
    placed = P("tm", "space", None, None)
    return jax.shard_map(
        per_device, mesh=mesh, in_specs=(placed,), out_specs=placed, check_vma=False
    )
```
